512 devices in a mesh: tm: 64 (over x, y, z_lo), head: 8 (over z_hi, core).
Axes of the slice: x: 4, y: 4, z: 16 (z_hi: 4, z_lo: 4; z = z_hi * 4 + z_lo), core: 2. Of those that a mesh axis runs over, the one named last changes fastest.
Arguments:
- query: bfloat16 [32768, 5120], P('tm', 'head'), may hold values from -100 to 100
- key: bfloat16 [32768, 5120], P('tm', 'head'), may hold values from -100 to 100
- value: bfloat16 [32768, 5120], P('tm', 'head'), may hold values from -6 to 6
- q_gain: float32 [5120], P('head'), may hold values from 0.1 to 1.9
- k_gain: float32 [5120], P('head'), may hold values from 0.1 to 1.9
- far_frames: int32 [512, 12], replicated, may hold values from -1 to 63, as said below
- far_pick: int32 [64, 64], replicated, may hold values from 0 to 7
Outputs:
- attended: bfloat16 [32768, 5120], P('tm', 'head')
The draws below stay inside these ranges and needn't reach their ends.
Inputs may be any that keep to these rules, and one draw needn't show every extreme that they name: `far_frames`: for query block r of frame f, entry j - 1 (j = 1 to 6) is a frame f - d and entry 5 + j a frame f + d, with 2**j <= d < 2**(j+1), or -1 where no frame of the video lies at such a distance on that side. In the first query block of each frame every such entry is the farthest frame that the band allows on that side.
All inputs are finite; a program needn't handle non-finite values.
Results may differ from the reference program's by a relative error of at most 0.012.
The reference program's roundings to bfloat16 on the way count: a program that leaves them out, or rounds other values in their place, can miss the bound.
Values may be sent and summed in bfloat16 or wider, within the bound.
A program may use at most 128 MiB of HBM per device.

```python
import jax
import jax.numpy as jnp
from jax import lax

HEADS = 40
HEAD_DIM = 128
D = 5120
TOK_FRAME = 512
BLOCK = 64
NFAR = 12
FRAMES = 64
TOKENS = 32768


def spread_rows(key):
    row_key, col_key, base_key = jax.random.split(key, 3)
    row_scale = jnp.exp(jax.random.uniform(row_key, (TOKENS, 1), jnp.float32, 0.0, 2.3))
    col_scale = jnp.exp(jax.random.uniform(col_key, (1, D), jnp.float32, 0.0, 2.3))
    base = jax.random.truncated_normal(base_key, -3.0, 3.0, (TOKENS, D), jnp.float32)
    return base * row_scale * col_scale / 3.0


def draw_query(key, part):
    key = jax.random.fold_in(key, 1)
    values = spread_rows(key)
    return values.astype(jnp.bfloat16)


def draw_key(key, part):
    key = jax.random.fold_in(key, 2)
    values = spread_rows(key)
    return values.astype(jnp.bfloat16)


def draw_far_frames(key, part):
    key = jax.random.fold_in(key, 3)
    block_total = TOKENS // BLOCK
    per_frame = TOK_FRAME // BLOCK
    frame = jnp.arange(block_total, dtype=jnp.int32) // per_frame
    first_block = (jnp.arange(block_total, dtype=jnp.int32) % per_frame == 0)[:, None]
    raw = jax.random.randint(key, (block_total, NFAR), 0, 2 ** 20, jnp.int32)
    half_slots = NFAR // 2
    slot = jnp.arange(NFAR, dtype=jnp.int32)
    band = slot % half_slots + 1
    side = jnp.where(slot < half_slots, -1, 1)
    lowest = jnp.left_shift(1, band)[None, :]
    highest = 2 * lowest - 1
    reach = jnp.where(side[None, :] < 0, frame[:, None], FRAMES - 1 - frame[:, None])
    upper = jnp.minimum(highest, reach)
    width_band = upper - lowest + 1
    distance = lowest + raw % jnp.maximum(width_band, 1)
    distance = jnp.where(first_block, upper, distance)
    target = frame[:, None] + side[None, :] * distance
    return jnp.where(width_band > 0, target, -1).astype(jnp.int32)


def draw_far_pick(key, part):
    key = jax.random.fold_in(key, 5)
    return jax.random.randint(key, (FRAMES, FRAMES), 0, TOK_FRAME // BLOCK, jnp.int32)


def levels(rng, shape, shards, low, high):
    loudness = 1.0
    for position, blocks in shards:
        heights = jax.random.uniform(jax.random.fold_in(jax.random.fold_in(rng, 6), position), (blocks,), jnp.float32, low / len(shards), high / len(shards))
        loudness = loudness * jnp.repeat(jnp.exp(heights), shape[position] // blocks).reshape((-1,) + (1,) * (len(shape) - 1 - position))
    return loudness


def centred(own_key, extent, scale, most, cuts=(), kind=jnp.bfloat16):
    drawn = jax.random.normal(own_key, extent, jnp.float32) * scale
    if len(cuts) > 0:
        drawn = levels(own_key, extent, cuts, -0.22, 0.18) * drawn
    return jnp.clip(drawn, min=-most, max=most).astype(kind)


def setup_inputs(seed: int = 0) -> dict:
    keys = jax.random.split(jax.random.key(seed), 8)
    return {
        "query": draw_query(jax.random.fold_in(keys[7], 71), 0),
        "key": draw_key(jax.random.fold_in(keys[7], 71), 0),
        "value": centred(keys[2], (TOKENS, D), 1.0, 6.0, ((0, 64), (1, 8))),
        "q_gain": jnp.clip(1.0 + 0.18 * jax.random.normal(keys[3], (D,), jnp.float32), 0.1, 1.9),
        "k_gain": jnp.clip(1.0 + 0.18 * jax.random.normal(keys[4], (D,), jnp.float32), 0.1, 1.9),
        "far_frames": draw_far_frames(jax.random.fold_in(keys[7], 71), 0),
        "far_pick": draw_far_pick(jax.random.fold_in(keys[7], 71), 0),
    }


epsilon = 1e-06
masked = -1e+30

def normalize(values, gain):
    squares = lax.optimization_barrier(jnp.sum(jnp.square(values.astype(jnp.float32)), axis=1))
    scaled = values.astype(jnp.float32) * lax.rsqrt(squares / D + epsilon)[:, None] * gain[None, :]
    return scaled.astype(jnp.bfloat16)

def reference(query, key, value, q_gain, k_gain, far_frames, far_pick):
    q_norm = normalize(query, q_gain)
    k_norm = normalize(key, k_gain)
    frame_count = TOKENS // TOK_FRAME
    block_count = TOK_FRAME // BLOCK
    key_pad = jnp.pad(k_norm, ((TOK_FRAME, TOK_FRAME), (0, 0)))
    value_pad = jnp.pad(value, ((TOK_FRAME, TOK_FRAME), (0, 0)))
    score_scale = HEAD_DIM ** (-0.5)

    def one_frame(frame):
        q_rows = lax.dynamic_slice_in_dim(q_norm, frame * TOK_FRAME, TOK_FRAME, 0).astype(jnp.float32)
        q_rows = q_rows.reshape(TOK_FRAME, HEADS, HEAD_DIM)
        near_key = lax.dynamic_slice_in_dim(key_pad, frame * TOK_FRAME, 3 * TOK_FRAME, 0).astype(jnp.float32)
        near_key = near_key.reshape(3 * TOK_FRAME, HEADS, HEAD_DIM)
        near_value = lax.dynamic_slice_in_dim(value_pad, frame * TOK_FRAME, 3 * TOK_FRAME, 0).astype(jnp.float32)
        near_value = near_value.reshape(3 * TOK_FRAME, HEADS, HEAD_DIM)
        key_frame = frame - 1 + jnp.arange(3 * TOK_FRAME) // TOK_FRAME
        near_ok = (key_frame >= 0) & (key_frame < frame_count)
        lists = lax.dynamic_slice_in_dim(far_frames, frame * block_count, block_count, 0)
        list_ok = lists >= 0
        sources = jnp.maximum(lists, 0).astype(jnp.int32)
        pick_row = lax.dynamic_index_in_dim(far_pick, frame, 0, keepdims=False)
        picked = jnp.take(pick_row, sources)
        offsets = (sources * TOK_FRAME + picked * BLOCK)[:, :, None] + jnp.arange(BLOCK)[None, None, :]
        offsets = offsets.reshape(block_count, NFAR * BLOCK).astype(jnp.int32)
        far_key = jnp.take(k_norm, offsets, axis=0).astype(jnp.float32)
        far_key = far_key.reshape(block_count, NFAR * BLOCK, HEADS, HEAD_DIM)
        far_value = jnp.take(value, offsets, axis=0).astype(jnp.float32)
        far_value = far_value.reshape(block_count, NFAR * BLOCK, HEADS, HEAD_DIM)
        far_ok = jnp.repeat(list_ok, BLOCK, axis=1)
        near_score = jnp.einsum('qhd,khd->hqk', q_rows, near_key) * score_scale
        near_score = jnp.where(near_ok[None, None, :], near_score, masked)
        near_score = near_score.reshape(HEADS, block_count, BLOCK, 3 * TOK_FRAME)
        q_blocks = q_rows.reshape(block_count, BLOCK, HEADS, HEAD_DIM)
        far_score = jnp.einsum('bqhd,bkhd->hbqk', q_blocks, far_key) * score_scale
        far_score = jnp.where(far_ok[None, :, None, :], far_score, masked)
        row_peak = jnp.maximum(near_score.max(-1), far_score.max(-1))[..., None]
        near_prob = jnp.exp(near_score - row_peak)
        far_prob = jnp.exp(far_score - row_peak)
        prob_sum = near_prob.sum(-1) + far_prob.sum(-1)
        near_weight = lax.optimization_barrier(near_prob.astype(jnp.bfloat16)).astype(jnp.float32)
        far_weight = lax.optimization_barrier(far_prob.astype(jnp.bfloat16)).astype(jnp.float32)
        near_out = jnp.einsum('hbqk,khd->bqhd', near_weight, near_value)
        far_out = jnp.einsum('hbqk,bkhd->bqhd', far_weight, far_value)
        divisor = jnp.transpose(prob_sum, (1, 2, 0))[..., None]
        result = ((near_out + far_out) / divisor).astype(jnp.bfloat16)
        return result.reshape(TOK_FRAME, D)
    return lax.map(one_frame, jnp.arange(frame_count)).reshape(TOKENS, D)
```

```python
import functools

import jax
import jax.numpy as jnp
from jax import lax
from jax.experimental import pallas as pl
from jax.experimental.pallas import tpu as pltpu
from jax.sharding import PartitionSpec as P

HEAD_DIM = 128
BLOCK = 64
NFAR = 12
SIDE = 4
HEADS = 5
BLOCKS = 8
FRAMES = 64
GROUPS = 8
TOK = BLOCK * BLOCKS
WIDTH = HEADS * HEAD_DIM
FULL = WIDTH * GROUPS
SLOTS = (0, 1, 2, 3, 4, 6, 7, 8, 9, 10)
FARK = len(SLOTS) * BLOCK
NEARK = 3 * TOK
epsilon = 1e-06
masked = -1e30
MESH = pl.DeviceIdType.MESH
PLANE = (
    (1, 0), (0, 1), (3, 0), (0, 3), (2, 0), (0, 2), (1, 1), (3, 3),
    (1, 3), (3, 1), (2, 1), (1, 2), (2, 3), (3, 2), (2, 2),
)
PEERS = len(PLANE)


def spread_kernel(
    q, k, v, qg, kg, pick, qn_o, near_o, far_o,
    zbuf, out, own, nbuf, sums, parts,
    zs, zr, fs, fr, ns, nr, hs, hr, ls,
):
    frame = lax.axis_index("tm")
    group = lax.axis_index("head")
    col, z = frame // SIDE, frame % SIDE
    x, y = col // SIDE, col % SIDE

    def tm(dev):
        return {"tm": dev}

    def plane_peer(d):
        return (((x + d[0]) % SIDE) * SIDE + (y + d[1]) % SIDE) * SIDE + z

    has_next, has_prev = col < 15, col > 0
    from_prev = jnp.logical_and(z == 0, has_prev)
    from_next = jnp.logical_and(z == SIDE - 1, has_next)
    next_dev = (col + 1) * SIDE
    prev_dev = (col - 1) * SIDE + SIDE - 1

    barrier = pltpu.get_barrier_semaphore()

    def greet(dev):
        pl.semaphore_signal(barrier, inc=1, device_id=dev, device_id_type=MESH)

    for d in PLANE:
        greet(tm(plane_peer(d)))
    for j in range(1, GROUPS):
        greet({"head": (group + j) % GROUPS})

    @pl.when(z > 0)
    def _():
        greet(tm(frame - 1))

    @pl.when(z < SIDE - 1)
    def _():
        greet(tm(frame + 1))

    @pl.when(has_next)
    def _():
        greet(tm(next_dev))

    @pl.when(has_prev)
    def _():
        greet(tm(prev_dev))

    @pl.when(from_prev)
    def _():
        for j in range(SIDE):
            greet(tm((col - 1) * SIDE + j))

    @pl.when(from_next)
    def _():
        for j in range(SIDE):
            greet(tm((col + 1) * SIDE + j))

    for h in range(HEADS):
        zbuf[0, z, h] = v[:, h * HEAD_DIM:(h + 1) * HEAD_DIM].reshape(BLOCKS, BLOCK, HEAD_DIM)
    lane = lax.broadcasted_iota(jnp.int32, (TOK, HEAD_DIM), 1)
    q_part = jnp.sum(jnp.square(q[...].astype(jnp.float32)), axis=1, keepdims=True)
    k_part = jnp.sum(jnp.square(k[...].astype(jnp.float32)), axis=1, keepdims=True)
    both = jnp.where(lane == 0, q_part, jnp.where(lane == 1, k_part, 0.0))
    sums[...] = jnp.transpose(both)[:8]

    lacks_near = jnp.logical_or(frame == 0, frame == FRAMES - 1)

    @pl.when(lacks_near)
    def _():
        nbuf[...] = jnp.zeros_like(nbuf)

    greeted = PEERS + GROUPS - 1
    for cond, n in (
        (z > 0, 1), (z < SIDE - 1, 1), (has_next, 1), (has_prev, 1),
        (from_prev, SIDE), (from_next, SIDE),
    ):
        greeted = greeted + jnp.where(cond, n, 0)
    pl.semaphore_wait(barrier, greeted)

    sum_copies = []
    for j in range(1, GROUPS):
        c = pltpu.make_async_remote_copy(
            sums, parts.at[j], hs.at[j], hr.at[j],
            device_id={"head": (group + j) % GROUPS}, device_id_type=MESH)
        c.start()
        sum_copies.append(c)

    def z_copy(t, j, hop, right):
        dev = frame + 1 if right else frame - 1
        return pltpu.make_async_remote_copy(
            zbuf.at[t, j], zbuf.at[t, j], zs.at[int(right), hop, t], zr.at[j, t],
            device_id=tm(dev), device_id_type=MESH)

    def near_copy(t, up):
        part = pl.ds(2 * z, 2)
        return pltpu.make_async_remote_copy(
            zbuf.at[t, SIDE - 1 if up else 0, :, part], nbuf.at[t, :, part],
            ns.at[int(up), t], nr.at[t],
            device_id=tm(next_dev if up else prev_dev), device_id_type=MESH)

    def step_frame(s):
        if s == 0:
            return z
        if s == SIDE - 1:
            return jnp.where(z < 2, SIDE - 1, 0)
        table = {1: (1, 0, 3, 2), 2: (2, 2, 1, 1)}[s]
        r = jnp.int32(table[0])
        for i in range(1, SIDE):
            r = jnp.where(z == i, table[i], r)
        return r

    def far_copy(s, t, i, j):
        return pltpu.make_async_remote_copy(
            out.at[s, t, i], far_o.at[t, col * SIDE + j], fs.at[s, t], fr.at[s, t],
            device_id=tm(plane_peer(PLANE[i])), device_id_type=MESH)

    def round_(s, t):
        if s == 0:
            @pl.when(z < SIDE - 1)
            def _():
                z_copy(t, z, 0, True).start()

            @pl.when(z > 0)
            def _():
                z_copy(t, z, 0, False).start()
        else:
            @pl.when(z - s >= 0)
            def _():
                z_copy(t, z - s, s, True).wait_recv()

                @pl.when(z < SIDE - 1)
                def _():
                    z_copy(t, z - s, s, True).start()

            @pl.when(z + s < SIDE)
            def _():
                z_copy(t, z + s, s, False).wait_recv()

                @pl.when(z > 0)
                def _():
                    z_copy(t, z + s, s, False).start()

        @pl.when(jnp.logical_and(z == SIDE - 1 - s, has_next))
        def _():
            near_copy(t, True).start()

        @pl.when(jnp.logical_and(z == s, has_prev))
        def _():
            near_copy(t, False).start()

        j = step_frame(s)
        g = col * SIDE + j
        picks = [pick[plane_peer(d), g] for d in PLANE] + [pick[frame, g]]

        def one_head(h, _):
            blocks = [zbuf[t, j, h, b] for b in range(BLOCKS)]
            for i, p in enumerate(picks):
                level = blocks
                for bit in range(3):
                    odd = ((p // (1 << bit)) % 2) == 1
                    level = [jnp.where(odd, level[2 * m + 1], level[2 * m]) for m in range(len(level) // 2)]
                if i < PEERS:
                    out[s, t, i, h] = level[0]
                else:
                    own[t, j, h] = level[0]
            return _

        lax.fori_loop(0, HEADS, one_head, 0)
        for i in range(PEERS):
            far_copy(s, t, i, j).start()
        pltpu.make_async_copy(own.at[t, j], far_o.at[t, g], ls.at[0, s, t]).start()

    round_(0, 0)
    for c in sum_copies:
        c.wait()
    total = sums[...]
    for j in range(1, GROUPS):
        total = total + parts[j]
    total = jnp.concatenate([total, jnp.zeros((HEAD_DIM - 8, TOK), jnp.float32)], axis=0)
    scale = lax.rsqrt(jnp.transpose(total) / FULL + epsilon)
    q_scale, k_scale = scale[:, 0:1], scale[:, 1:2]
    for h in range(HEADS):
        cut = slice(h * HEAD_DIM, (h + 1) * HEAD_DIM)
        k_norm = (k[:, cut].astype(jnp.float32) * k_scale * kg[:, cut]).astype(jnp.bfloat16)
        zbuf[1, z, h] = k_norm.reshape(BLOCKS, BLOCK, HEAD_DIM)
        qn_o[h] = (q[:, cut].astype(jnp.float32) * q_scale * qg[:, cut]).astype(jnp.bfloat16)
    round_(0, 1)
    for s in range(1, SIDE):
        for t in range(2):
            round_(s, t)

    @pl.when(jnp.logical_or(from_prev, from_next))
    def _():
        for t in range(2):
            pltpu.make_async_copy(nbuf.at[t], nbuf.at[t], nr.at[t]).wait()

    def near_out(t, place, src):
        return pltpu.make_async_copy(src, near_o.at[t, place], ls.at[1, place, t])

    for t in range(2):
        near_out(t, 1, zbuf.at[t, z]).start()

        @pl.when(z > 0)
        def _():
            near_out(t, 0, zbuf.at[t, z - 1]).start()

        @pl.when(z == 0)
        def _():
            near_out(t, 0, nbuf.at[t]).start()

        @pl.when(z < SIDE - 1)
        def _():
            near_out(t, 2, zbuf.at[t, z + 1]).start()

        @pl.when(z == SIDE - 1)
        def _():
            near_out(t, 2, nbuf.at[t]).start()

    for t in range(2):
        for place in range(3):
            near_out(t, place, nbuf.at[t]).wait()
        for s in range(SIDE):
            pltpu.make_async_copy(own.at[t, 0], far_o.at[t, 0], ls.at[0, s, t]).wait()
            pltpu.make_async_copy(out.at[s, t], out.at[s, t], fs.at[s, t]).wait()
            pltpu.make_async_copy(out.at[s, t], out.at[s, t], fr.at[s, t]).wait()

            @pl.when(jnp.logical_and(z - s >= 0, z < SIDE - 1))
            def _():
                z_copy(t, z - s, s, True).wait_send()

            @pl.when(jnp.logical_and(z + s < SIDE, z > 0))
            def _():
                z_copy(t, z + s, s, False).wait_send()

        @pl.when(has_next)
        def _():
            near_copy(t, True).wait_send()

        @pl.when(has_prev)
        def _():
            near_copy(t, False).wait_send()


def spread(query, key, value, q_gain, k_gain, far_pick):
    vmem = pl.BlockSpec(memory_space=pltpu.VMEM)
    hbm = pl.BlockSpec(memory_space=pl.ANY)
    dma = pltpu.SemaphoreType.DMA
    bf = jnp.bfloat16
    return pl.pallas_call(
        spread_kernel,
        out_shape=(
            jax.ShapeDtypeStruct((HEADS, TOK, HEAD_DIM), bf),
            jax.ShapeDtypeStruct((2, 3, HEADS, BLOCKS, BLOCK, HEAD_DIM), bf),
            jax.ShapeDtypeStruct((2, FRAMES, HEADS, BLOCK, HEAD_DIM), bf),
        ),
        in_specs=[vmem] * 5 + [pl.BlockSpec(memory_space=pltpu.SMEM)],
        out_specs=(vmem, hbm, hbm),
        scratch_shapes=[
            pltpu.VMEM((2, SIDE, HEADS, BLOCKS, BLOCK, HEAD_DIM), bf),
            pltpu.VMEM((SIDE, 2, PEERS, HEADS, BLOCK, HEAD_DIM), bf),
            pltpu.VMEM((2, SIDE, HEADS, BLOCK, HEAD_DIM), bf),
            pltpu.VMEM((2, HEADS, BLOCKS, BLOCK, HEAD_DIM), bf),
            pltpu.VMEM((8, TOK), jnp.float32),
            pltpu.VMEM((GROUPS, 8, TOK), jnp.float32),
            dma((2, SIDE, 2)), dma((SIDE, 2)),
            dma((SIDE, 2)), dma((SIDE, 2)),
            dma((2, 2)), dma((2,)),
            dma((GROUPS,)), dma((GROUPS,)),
            dma((2, SIDE, 2)),
        ],
        compiler_params=pltpu.CompilerParams(
            collective_id=0, has_side_effects=True, vmem_limit_bytes=48 << 20),
    )(query, key, value, q_gain, k_gain, far_pick)


def attend_kernel(lists, q, near, far, o):
    tile = pl.program_id(1)
    rows = q.shape[1]
    per_tile = rows // BLOCK
    frame = lists[NFAR * BLOCKS]
    rate = HEAD_DIM ** (-0.5) * 1.4426950408889634
    keys = near[1, :, 0].reshape(NEARK, HEAD_DIM)
    vals = near[0, :, 0].reshape(NEARK, HEAD_DIM)
    dims = (((1,), (1,)), ((), ()))
    place = lax.broadcasted_iota(jnp.int32, (1, NEARK), 1) // TOK
    near_ok = jnp.logical_and(
        jnp.logical_or(place > 0, frame > 0), jnp.logical_or(place < 2, frame < FRAMES - 1))
    near_s = lax.dot_general(q[0], keys, dims, preferred_element_type=jnp.float32)
    near_s = jnp.where(near_ok, near_s, masked)
    slot = lax.broadcasted_iota(jnp.int32, (1, FARK), 1) // BLOCK
    far_s, picked = [], []
    for b in range(per_tile):
        sources = [lists[(tile * per_tile + b) * NFAR + s] for s in SLOTS]
        bias = jnp.zeros((1, FARK), jnp.float32)
        for i, g in enumerate(sources):
            bias = jnp.where(slot == i, jnp.where(g >= 0, 0.0, masked), bias)
        held = [jnp.maximum(g, 0) for g in sources]
        far_k = jnp.concatenate([far[1, g, 0] for g in held], axis=0)
        picked.append(held)
        far_s.append(lax.dot_general(
            q[0, b * BLOCK:(b + 1) * BLOCK], far_k, dims, preferred_element_type=jnp.float32) + bias)
    far_s = jnp.concatenate(far_s, axis=0)
    peak = jnp.maximum(near_s.max(-1, keepdims=True), far_s.max(-1, keepdims=True))
    near_p = jnp.exp2((near_s - peak) * rate)
    far_p = jnp.exp2((far_s - peak) * rate)
    total = near_p.sum(-1, keepdims=True) + far_p.sum(-1, keepdims=True)
    near_o = jnp.dot(near_p.astype(jnp.bfloat16), vals, preferred_element_type=jnp.float32)
    far_p = far_p.astype(jnp.bfloat16)
    far_o = []
    for b in range(per_tile):
        far_v = jnp.concatenate([far[0, g, 0] for g in picked[b]], axis=0)
        far_o.append(jnp.dot(
            far_p[b * BLOCK:(b + 1) * BLOCK], far_v, preferred_element_type=jnp.float32))
    o[...] = ((near_o + jnp.concatenate(far_o, axis=0)) / total).astype(jnp.bfloat16)


def attend(lists, q, near, far, rows=256):
    near = near.reshape(2, 3, HEADS, TOK, HEAD_DIM)
    return pl.pallas_call(
        attend_kernel,
        out_shape=jax.ShapeDtypeStruct((TOK, WIDTH), jnp.bfloat16),
        grid_spec=pltpu.PrefetchScalarGridSpec(
            num_scalar_prefetch=1,
            grid=(HEADS, TOK // rows),
            in_specs=[
                pl.BlockSpec((1, rows, HEAD_DIM), lambda h, i, _: (h, i, 0)),
                pl.BlockSpec((2, 3, 1, TOK, HEAD_DIM), lambda h, i, _: (0, 0, h, 0, 0)),
                pl.BlockSpec((2, FRAMES, 1, BLOCK, HEAD_DIM), lambda h, i, _: (0, 0, h, 0, 0)),
            ],
            out_specs=pl.BlockSpec((rows, HEAD_DIM), lambda h, i, _: (i, h)),
        ),
        compiler_params=pltpu.CompilerParams(vmem_limit_bytes=48 << 20),
    )(lists, q, near, far)


def local(query, key, value, q_gain, k_gain, far_frames, far_pick):
    frame = lax.axis_index("tm")
    mine = lax.dynamic_slice_in_dim(far_frames, frame * BLOCKS, BLOCKS, 0)
    lists = jnp.concatenate([mine.reshape(-1), frame.reshape(1).astype(jnp.int32)])
    q_norm, near, far = spread(
        query, key, value, q_gain.reshape(1, WIDTH), k_gain.reshape(1, WIDTH), far_pick)
    return attend(lists, q_norm, near, far)


def solution(mesh):
    placed = (P("tm", "head"), P("tm", "head"), P("tm", "head"), P("head"), P("head"), P(), P())
    return jax.shard_map(
        local, mesh=mesh, in_specs=placed, out_specs=P("tm", "head"), check_vma=False
    )
```

```python
import functools

import jax
import jax.numpy as jnp
from jax import lax
from jax.experimental import pallas as pl
from jax.experimental.pallas import tpu as pltpu
from jax.sharding import PartitionSpec as P

HEAD_DIM = 128
BLOCK = 64
NFAR = 12
SIDE = 4
HEADS = 5
BLOCKS = 8
FRAMES = 64
GROUPS = 8
TOK = BLOCK * BLOCKS
WIDTH = HEADS * HEAD_DIM
FULL = WIDTH * GROUPS
SLOTS = (0, 1, 2, 3, 4, 6, 7, 8, 9, 10)
FARK = len(SLOTS) * BLOCK
NEARK = 3 * TOK
epsilon = 1e-06
masked = -1e30
MESH = pl.DeviceIdType.MESH
PLANE = (
    (1, 0), (0, 1), (3, 0), (0, 3), (2, 0), (0, 2), (1, 1), (3, 3),
    (1, 3), (3, 1), (2, 1), (1, 2), (2, 3), (3, 2), (2, 2),
)
PEERS = len(PLANE)
HALF = 8
ROWS = 256
RATE = HEAD_DIM ** (-0.5) * 1.4426950408889634
DIMS = (((1,), (1,)), ((), ()))


def spread_kernel(
    q, k, v, qg, kg, pick, qn_o, acc_o, stat_o, far_o,
    q_in, k_in, qn, acc, stat, zbuf, out, own, nbuf, sums, parts,
    ins, zs, zr, fs, fr, ns, nr, hs, hr, ls, os,
):
    frame = lax.axis_index("tm")
    group = lax.axis_index("head")
    col, z = frame // SIDE, frame % SIDE
    x, y = col // SIDE, col % SIDE

    def tm(dev):
        return {"tm": dev}

    def plane_peer(d):
        return (((x + d[0]) % SIDE) * SIDE + (y + d[1]) % SIDE) * SIDE + z

    def cut(h):
        return slice(h * HEAD_DIM, (h + 1) * HEAD_DIM)

    has_next, has_prev = col < 15, col > 0
    from_prev = jnp.logical_and(z == 0, has_prev)
    from_next = jnp.logical_and(z == SIDE - 1, has_next)
    next_dev = (col + 1) * SIDE
    prev_dev = (col - 1) * SIDE + SIDE - 1

    loads = [pltpu.make_async_copy(q, q_in, ins.at[0]), pltpu.make_async_copy(k, k_in, ins.at[1])]
    loads += [pltpu.make_async_copy(v.at[:, cut(h)], zbuf.at[0, z, h], ins.at[2 + h]) for h in range(HEADS)]
    for c in loads:
        c.start()

    barrier = pltpu.get_barrier_semaphore()

    def greet(dev):
        pl.semaphore_signal(barrier, inc=1, device_id=dev, device_id_type=MESH)

    for d in PLANE:
        greet(tm(plane_peer(d)))
    for j in range(1, GROUPS):
        greet({"head": (group + j) % GROUPS})

    @pl.when(z > 0)
    def _():
        greet(tm(frame - 1))

    @pl.when(z < SIDE - 1)
    def _():
        greet(tm(frame + 1))

    @pl.when(has_next)
    def _():
        greet(tm(next_dev))

    @pl.when(has_prev)
    def _():
        greet(tm(prev_dev))

    @pl.when(from_prev)
    def _():
        for j in range(SIDE):
            greet(tm((col - 1) * SIDE + j))

    @pl.when(from_next)
    def _():
        for j in range(SIDE):
            greet(tm((col + 1) * SIDE + j))

    loads[0].wait()
    loads[1].wait()
    lane = lax.broadcasted_iota(jnp.int32, (TOK, HEAD_DIM), 1)
    q_part = jnp.sum(jnp.square(q_in[...].astype(jnp.float32)), axis=1, keepdims=True)
    k_part = jnp.sum(jnp.square(k_in[...].astype(jnp.float32)), axis=1, keepdims=True)
    both = jnp.where(lane == 0, q_part, jnp.where(lane == 1, k_part, 0.0))
    sums[...] = jnp.transpose(both)[:8]

    lacks_near = jnp.logical_or(frame == 0, frame == FRAMES - 1)

    @pl.when(lacks_near)
    def _():
        nbuf[...] = jnp.zeros_like(nbuf)

    for c in loads[2:]:
        c.wait()
    greeted = PEERS + GROUPS - 1
    for cond, n in (
        (z > 0, 1), (z < SIDE - 1, 1), (has_next, 1), (has_prev, 1),
        (from_prev, SIDE), (from_next, SIDE),
    ):
        greeted = greeted + jnp.where(cond, n, 0)
    pl.semaphore_wait(barrier, greeted)

    sum_copies = []
    for j in range(1, GROUPS):
        c = pltpu.make_async_remote_copy(
            sums, parts.at[j], hs.at[j], hr.at[j],
            device_id={"head": (group + j) % GROUPS}, device_id_type=MESH)
        c.start()
        sum_copies.append(c)

    def z_copy(t, j, hop, right):
        dev = frame + 1 if right else frame - 1
        return pltpu.make_async_remote_copy(
            zbuf.at[t, j], zbuf.at[t, j], zs.at[int(right), hop, t], zr.at[j, t],
            device_id=tm(dev), device_id_type=MESH)

    def near_copy(t, up):
        part = pl.ds(2 * BLOCK * z, 2 * BLOCK)
        return pltpu.make_async_remote_copy(
            zbuf.at[t, SIDE - 1 if up else 0, :, part], nbuf.at[t, :, part],
            ns.at[int(up), t], nr.at[t],
            device_id=tm(next_dev if up else prev_dev), device_id_type=MESH)

    def step_frame(s):
        if s == 0:
            return z
        if s == SIDE - 1:
            return jnp.where(z < 2, SIDE - 1, 0)
        table = {1: (1, 0, 3, 2), 2: (2, 2, 1, 1)}[s]
        r = jnp.int32(table[0])
        for i in range(1, SIDE):
            r = jnp.where(z == i, table[i], r)
        return r

    def far_copy(s, t, i, j):
        return pltpu.make_async_remote_copy(
            out.at[s, t, i], far_o.at[t, col * SIDE + j], fs.at[s, t, i // HALF], fr.at[s, t],
            device_id=tm(plane_peer(PLANE[i])), device_id_type=MESH)

    def sent(s, t, half):
        part = out.at[s, t, pl.ds(half * HALF, HALF if half == 0 else PEERS - HALF)]
        return pltpu.make_async_copy(part, part, fs.at[s, t, half])

    def column(s, t):
        if s == 0:
            @pl.when(z < SIDE - 1)
            def _():
                z_copy(t, z, 0, True).start()

            @pl.when(z > 0)
            def _():
                z_copy(t, z, 0, False).start()
        else:
            @pl.when(z - s >= 0)
            def _():
                z_copy(t, z - s, s, True).wait_recv()

                @pl.when(z < SIDE - 1)
                def _():
                    z_copy(t, z - s, s, True).start()

            @pl.when(z + s < SIDE)
            def _():
                z_copy(t, z + s, s, False).wait_recv()

                @pl.when(z > 0)
                def _():
                    z_copy(t, z + s, s, False).start()

        @pl.when(jnp.logical_and(z == SIDE - 1 - s, has_next))
        def _():
            near_copy(t, True).start()

        @pl.when(jnp.logical_and(z == s, has_prev))
        def _():
            near_copy(t, False).start()

    def choose(s, t):
        j = step_frame(s)
        g = col * SIDE + j
        picks = [pick[plane_peer(d), g] for d in PLANE] + [pick[frame, g]]

        def one_head(h, carry):
            blocks = [zbuf[t, j, h, b * BLOCK:(b + 1) * BLOCK] for b in range(BLOCKS)]
            for i, p in enumerate(picks):
                level = blocks
                for bit in range(3):
                    odd = ((p // (1 << bit)) % 2) == 1
                    level = [jnp.where(odd, level[2 * m + 1], level[2 * m]) for m in range(len(level) // 2)]
                if i < PEERS:
                    out[s, t, i, h] = level[0]
                else:
                    own[t, j, h] = level[0]
            return carry

        lax.fori_loop(0, HEADS, one_head, 0)
        pltpu.make_async_copy(own.at[t, j], far_o.at[t, g], ls.at[s, t]).start()

    def post(s, t, half):
        j = step_frame(s)
        for i in range(PEERS):
            if i // HALF == half:
                far_copy(s, t, i, j).start()

    column(0, 0)
    choose(0, 0)
    post(0, 0, 0)
    post(0, 0, 1)
    for c in sum_copies:
        c.wait()
    total = sums[...]
    for j in range(1, GROUPS):
        total = total + parts[j]
    total = jnp.concatenate([total, jnp.zeros((HEAD_DIM - 8, TOK), jnp.float32)], axis=0)
    scale = lax.rsqrt(jnp.transpose(total) / FULL + epsilon)
    q_scale, k_scale = scale[:, 0:1], scale[:, 1:2]
    for h in range(HEADS):
        k_norm = k_in[:, cut(h)].astype(jnp.float32) * k_scale * kg[:, cut(h)]
        zbuf[1, z, h] = k_norm.astype(jnp.bfloat16)
    column(0, 1)
    for h in range(HEADS):
        qn[h] = (q_in[:, cut(h)].astype(jnp.float32) * q_scale * qg[:, cut(h)]).astype(jnp.bfloat16)
    q_out = pltpu.make_async_copy(qn, qn_o, os.at[0])
    q_out.start()
    order = [(s, t) for s in range(SIDE) for t in range(2)]
    for r in range(1, len(order)):
        s, t = order[r]
        choose(s, t)
        sent(*order[r - 1], 0).wait()
        post(s, t, 0)
        if r + 1 < len(order):
            column(*order[r + 1])
        sent(*order[r - 1], 1).wait()
        post(s, t, 1)

    @pl.when(jnp.logical_or(from_prev, from_next))
    def _():
        for t in range(2):
            pltpu.make_async_copy(nbuf.at[t], nbuf.at[t], nr.at[t]).wait()

    def near_rows(t, h):
        prev = jnp.where(z > 0, zbuf[t, jnp.maximum(z - 1, 0), h], nbuf[t, h])
        after = jnp.where(z < SIDE - 1, zbuf[t, jnp.minimum(z + 1, SIDE - 1), h], nbuf[t, h])
        return jnp.concatenate([prev, zbuf[t, z, h], after], axis=0)

    place = lax.broadcasted_iota(jnp.int32, (1, NEARK), 1) // TOK
    near_ok = jnp.logical_and(
        jnp.logical_or(place > 0, frame > 0), jnp.logical_or(place < 2, frame < FRAMES - 1))
    half_lane = lax.broadcasted_iota(jnp.int32, (ROWS, HEAD_DIM), 1) < BLOCK

    def near_tile(n, carry):
        h, i = n // (TOK // ROWS), n % (TOK // ROWS)
        rows = pl.ds(i * ROWS, ROWS)
        score = lax.dot_general(qn[h, rows], near_rows(1, h), DIMS, preferred_element_type=jnp.float32)
        score = jnp.where(near_ok, score, masked)
        peak = score.max(-1, keepdims=True)
        prob = jnp.exp2((score - peak) * RATE)
        total = prob.sum(-1, keepdims=True)
        acc[h, rows] = jnp.dot(
            prob.astype(jnp.bfloat16), near_rows(0, h), preferred_element_type=jnp.float32)
        stat[h, rows] = jnp.where(half_lane, peak, total)
        return carry

    lax.fori_loop(0, HEADS * (TOK // ROWS), near_tile, 0)
    near_out = [pltpu.make_async_copy(acc, acc_o, os.at[1]), pltpu.make_async_copy(stat, stat_o, os.at[2])]
    for c in near_out:
        c.start()

    for t in range(2):
        for s in range(SIDE):
            pltpu.make_async_copy(own.at[t, 0], far_o.at[t, 0], ls.at[s, t]).wait()
            pltpu.make_async_copy(out.at[s, t], out.at[s, t], fr.at[s, t]).wait()

            @pl.when(jnp.logical_and(z - s >= 0, z < SIDE - 1))
            def _():
                z_copy(t, z - s, s, True).wait_send()

            @pl.when(jnp.logical_and(z + s < SIDE, z > 0))
            def _():
                z_copy(t, z + s, s, False).wait_send()

        @pl.when(has_next)
        def _():
            near_copy(t, True).wait_send()

        @pl.when(has_prev)
        def _():
            near_copy(t, False).wait_send()
    sent(*order[-1], 0).wait()
    sent(*order[-1], 1).wait()
    q_out.wait()
    for c in near_out:
        c.wait()


def spread(query, key, value, q_gain, k_gain, far_pick):
    vmem = pl.BlockSpec(memory_space=pltpu.VMEM)
    hbm = pl.BlockSpec(memory_space=pl.ANY)
    dma = pltpu.SemaphoreType.DMA
    bf, f32 = jnp.bfloat16, jnp.float32
    heads = (HEADS, TOK, HEAD_DIM)
    return pl.pallas_call(
        spread_kernel,
        out_shape=(
            jax.ShapeDtypeStruct(heads, bf),
            jax.ShapeDtypeStruct(heads, f32),
            jax.ShapeDtypeStruct(heads, f32),
            jax.ShapeDtypeStruct((2, FRAMES, HEADS, BLOCK, HEAD_DIM), bf),
        ),
        in_specs=[hbm] * 3 + [vmem] * 2 + [pl.BlockSpec(memory_space=pltpu.SMEM)],
        out_specs=(hbm,) * 4,
        scratch_shapes=[
            pltpu.VMEM((TOK, WIDTH), bf),
            pltpu.VMEM((TOK, WIDTH), bf),
            pltpu.VMEM(heads, bf),
            pltpu.VMEM(heads, f32),
            pltpu.VMEM(heads, f32),
            pltpu.VMEM((2, SIDE) + heads, bf),
            pltpu.VMEM((SIDE, 2, PEERS, HEADS, BLOCK, HEAD_DIM), bf),
            pltpu.VMEM((2, SIDE, HEADS, BLOCK, HEAD_DIM), bf),
            pltpu.VMEM((2,) + heads, bf),
            pltpu.VMEM((8, TOK), f32),
            pltpu.VMEM((GROUPS, 8, TOK), f32),
            dma((2 + HEADS,)),
            dma((2, SIDE, 2)), dma((SIDE, 2)),
            dma((SIDE, 2, 2)), dma((SIDE, 2)),
            dma((2, 2)), dma((2,)),
            dma((GROUPS,)), dma((GROUPS,)),
            dma((SIDE, 2)), dma((3,)),
        ],
        compiler_params=pltpu.CompilerParams(
            collective_id=0, has_side_effects=True, vmem_limit_bytes=48 << 20),
    )(query, key, value, q_gain, k_gain, far_pick)


def attend_kernel(lists, q, acc, stat, far, o):
    slot = lax.broadcasted_iota(jnp.int32, (1, FARK), 1) // BLOCK
    scores, picked = [], []
    for b in range(BLOCKS):
        sources = [lists[b * NFAR + s] for s in SLOTS]
        bias = jnp.zeros((1, FARK), jnp.float32)
        for i, g in enumerate(sources):
            bias = jnp.where(slot == i, jnp.where(g >= 0, 0.0, masked), bias)
        held = [jnp.maximum(g, 0) for g in sources]
        far_k = jnp.concatenate([far[1, g, 0] for g in held], axis=0)
        picked.append(held)
        scores.append(lax.dot_general(
            q[0, b * BLOCK:(b + 1) * BLOCK], far_k, DIMS, preferred_element_type=jnp.float32) + bias)
    for b in range(BLOCKS):
        rows = slice(b * BLOCK, (b + 1) * BLOCK)
        near_peak, near_total = stat[0, rows, 0:1], stat[0, rows, BLOCK:BLOCK + 1]
        peak = jnp.maximum(near_peak, scores[b].max(-1, keepdims=True))
        prob = jnp.exp2((scores[b] - peak) * RATE)
        shrink = jnp.exp2((near_peak - peak) * RATE)
        total = near_total * shrink + prob.sum(-1, keepdims=True)
        far_v = jnp.concatenate([far[0, g, 0] for g in picked[b]], axis=0)
        sums = acc[0, rows] * shrink + jnp.dot(
            prob.astype(jnp.bfloat16), far_v, preferred_element_type=jnp.float32)
        o[rows] = (sums / total).astype(jnp.bfloat16)


def attend(lists, q, acc, stat, far):
    head = pl.BlockSpec((1, TOK, HEAD_DIM), lambda h, _: (h, 0, 0))
    return pl.pallas_call(
        attend_kernel,
        out_shape=jax.ShapeDtypeStruct((TOK, WIDTH), jnp.bfloat16),
        grid_spec=pltpu.PrefetchScalarGridSpec(
            num_scalar_prefetch=1,
            grid=(HEADS,),
            in_specs=[head] * 3 + [
                pl.BlockSpec((2, FRAMES, 1, BLOCK, HEAD_DIM), lambda h, _: (0, 0, h, 0, 0)),
            ],
            out_specs=pl.BlockSpec((TOK, HEAD_DIM), lambda h, _: (0, h)),
        ),
        compiler_params=pltpu.CompilerParams(vmem_limit_bytes=48 << 20),
    )(lists, q, acc, stat, far)


def local(query, key, value, q_gain, k_gain, far_frames, far_pick):
    frame = lax.axis_index("tm")
    mine = lax.dynamic_slice_in_dim(far_frames, frame * BLOCKS, BLOCKS, 0)
    held = spread(
        query, key, value, q_gain.reshape(1, WIDTH), k_gain.reshape(1, WIDTH), far_pick)
    return attend(mine.reshape(-1), *held)


def solution(mesh):
    placed = (P("tm", "head"), P("tm", "head"), P("tm", "head"), P("head"), P("head"), P(), P())
    return jax.shard_map(
        local, mesh=mesh, in_specs=placed, out_specs=P("tm", "head"), check_vma=False
    )
```

```python
import functools

import jax
import jax.numpy as jnp
from jax import lax
from jax.experimental import pallas as pl
from jax.experimental.pallas import tpu as pltpu
from jax.sharding import PartitionSpec as P

HEAD_DIM = 128
BLOCK = 64
NFAR = 12
SIDE = 4
HEADS = 5
BLOCKS = 8
FRAMES = 64
GROUPS = 8
TOK = BLOCK * BLOCKS
WIDTH = HEADS * HEAD_DIM
FULL = WIDTH * GROUPS
SLOTS = (0, 1, 2, 3, 4, 6, 7, 8, 9, 10)
FARK = len(SLOTS) * BLOCK
NEARK = 3 * TOK
epsilon = 1e-06
masked = -1e30
MESH = pl.DeviceIdType.MESH
PLANE = (
    (1, 0), (0, 1), (3, 0), (0, 3), (2, 0), (0, 2), (1, 1), (3, 3),
    (1, 3), (3, 1), (2, 1), (1, 2), (2, 3), (3, 2), (2, 2),
)
PEERS = len(PLANE)
HALF = 8
ROWS = 256
RATE = HEAD_DIM ** (-0.5) * 1.4426950408889634
DIMS = (((1,), (1,)), ((), ()))


def spread_kernel(
    q, k, v, qg, kg, pick, qn_o, acc_o, stat_o, far_o,
    q_in, k_in, qn, acc, stat, zbuf, out, own, stage, nbuf, sums, parts,
    ins, zs, zr, fs, fr, ns, yr, cs, nr, hs, hr, ls, os,
):
    frame = lax.axis_index("tm")
    group = lax.axis_index("head")
    col, z = frame // SIDE, frame % SIDE
    x, y = col // SIDE, col % SIDE

    def tm(dev):
        return {"tm": dev}

    def plane_peer(d):
        return (((x + d[0]) % SIDE) * SIDE + (y + d[1]) % SIDE) * SIDE + z

    def cut(h):
        return slice(h * HEAD_DIM, (h + 1) * HEAD_DIM)

    has_next, has_prev = col < 15, col > 0
    from_prev = jnp.logical_and(z == 0, has_prev)
    from_next = jnp.logical_and(z == SIDE - 1, has_next)

    loads = [pltpu.make_async_copy(q, q_in, ins.at[0]), pltpu.make_async_copy(k, k_in, ins.at[1])]
    loads += [pltpu.make_async_copy(v.at[:, cut(h)], zbuf.at[0, z, h], ins.at[2 + h]) for h in range(HEADS)]
    for c in loads:
        c.start()

    barrier = pltpu.get_barrier_semaphore()

    def greet(dev):
        pl.semaphore_signal(barrier, inc=1, device_id=dev, device_id_type=MESH)

    for d in PLANE:
        greet(tm(plane_peer(d)))
    for j in range(1, GROUPS):
        greet({"head": (group + j) % GROUPS})

    for j in range(1, SIDE):
        greet(tm(col * SIDE + (z + j) % SIDE))

    loads[0].wait()
    loads[1].wait()
    lane = lax.broadcasted_iota(jnp.int32, (TOK, HEAD_DIM), 1)
    q_part = jnp.sum(jnp.square(q_in[...].astype(jnp.float32)), axis=1, keepdims=True)
    k_part = jnp.sum(jnp.square(k_in[...].astype(jnp.float32)), axis=1, keepdims=True)
    both = jnp.where(lane == 0, q_part, jnp.where(lane == 1, k_part, 0.0))
    sums[...] = jnp.transpose(both)[:8]

    for c in loads[2:]:
        c.wait()
    pl.semaphore_wait(barrier, PEERS + GROUPS - 1 + SIDE - 1)

    sum_copies = []
    for j in range(1, GROUPS):
        c = pltpu.make_async_remote_copy(
            sums, parts.at[j], hs.at[j], hr.at[j],
            device_id={"head": (group + j) % GROUPS}, device_id_type=MESH)
        c.start()
        sum_copies.append(c)

    def z_copy(t, j, hop, right, h=None):
        dev = frame + 1 if right else frame - 1
        part = zbuf.at[t, j] if h is None else zbuf.at[t, j, h]
        return pltpu.make_async_remote_copy(
            part, part, zs.at[int(right), hop, t], zr.at[j, t],
            device_id=tm(dev), device_id_type=MESH)

    quarter = pl.ds(2 * BLOCK * z, 2 * BLOCK)
    over = (has_prev, has_next)
    goal = (0, SIDE - 1)

    def near_copy(t, up, h=None):
        heads = slice(None) if h is None else h
        return pltpu.make_async_remote_copy(
            zbuf.at[t, SIDE - 1 if up else 0, heads, quarter], stage.at[1 - up, t, heads],
            ns.at[up, t], yr.at[1 - up, t],
            device_id=tm(frame + SIDE if up else frame - SIDE), device_id_type=MESH)

    def cross(t):
        for h in range(HEADS):
            for up in (1, 0):
                @pl.when(over[up])
                def _():
                    near_copy(t, up, h).start()

    def last_copy(t, way):
        return pltpu.make_async_remote_copy(
            stage.at[way, t], nbuf.at[t, :, quarter], cs.at[way, t], nr.at[t],
            device_id=tm(col * SIDE + goal[way]), device_id_type=MESH)

    def deliver(t):
        for way in (0, 1):
            @pl.when(over[way])
            def _():
                pltpu.make_async_copy(stage.at[way, t], stage.at[way, t], yr.at[way, t]).wait()

                @pl.when(z != goal[way])
                def _():
                    last_copy(t, way).start()

                @pl.when(z == goal[way])
                def _():
                    pltpu.make_async_copy(stage.at[way, t], nbuf.at[t, :, quarter], nr.at[t]).start()

    def step_frame(s):
        if s == 0:
            return z
        if s == SIDE - 1:
            return jnp.where(z < 2, SIDE - 1, 0)
        table = {1: (1, 0, 3, 2), 2: (2, 2, 1, 1)}[s]
        r = jnp.int32(table[0])
        for i in range(1, SIDE):
            r = jnp.where(z == i, table[i], r)
        return r

    def far_copy(s, t, i, j):
        return pltpu.make_async_remote_copy(
            out.at[s, t, i], far_o.at[t, col * SIDE + j], fs.at[s, t, i // HALF], fr.at[s, t],
            device_id=tm(plane_peer(PLANE[i])), device_id_type=MESH)

    def sent(s, t, half):
        part = out.at[s, t, pl.ds(half * HALF, HALF if half == 0 else PEERS - HALF)]
        return pltpu.make_async_copy(part, part, fs.at[s, t, half])

    def arrive(s, t):
        @pl.when(z - s >= 0)
        def _():
            z_copy(t, z - s, s, True).wait_recv()

        @pl.when(z + s < SIDE)
        def _():
            z_copy(t, z + s, s, False).wait_recv()

    def column(s, t, h):
        @pl.when(jnp.logical_and(z - s >= 0, z < SIDE - 1))
        def _():
            z_copy(t, z - s, s, True, h).start()

        @pl.when(jnp.logical_and(z + s < SIDE, z > 0))
        def _():
            z_copy(t, z + s, s, False, h).start()

    def choose(s, t):
        j = step_frame(s)
        g = col * SIDE + j
        picks = [pick[plane_peer(d), g] for d in PLANE] + [pick[frame, g]]

        def one_head(h, carry):
            blocks = [zbuf[t, j, h, b * BLOCK:(b + 1) * BLOCK] for b in range(BLOCKS)]
            for i, p in enumerate(picks):
                level = blocks
                for bit in range(3):
                    odd = ((p // (1 << bit)) % 2) == 1
                    level = [jnp.where(odd, level[2 * m + 1], level[2 * m]) for m in range(len(level) // 2)]
                if i < PEERS:
                    out[s, t, i, h] = level[0]
                else:
                    own[t, j, h] = level[0]
            return carry

        lax.fori_loop(0, HEADS, one_head, 0)
        pltpu.make_async_copy(own.at[t, j], far_o.at[t, g], ls.at[s, t]).start()

    def post(s, t, half, beside=None):
        j = step_frame(s)
        for i in range(PEERS):
            if i // HALF == half:
                far_copy(s, t, i, j).start()
                if beside is not None and i % HALF < HEADS:
                    column(*beside, i % HALF)

    for h in range(HEADS):
        column(0, 0, h)
    choose(0, 0)
    post(0, 0, 0)
    post(0, 0, 1)
    for c in sum_copies:
        c.wait()
    total = sums[...]
    for j in range(1, GROUPS):
        total = total + parts[j]
    total = jnp.concatenate([total, jnp.zeros((HEAD_DIM - 8, TOK), jnp.float32)], axis=0)
    scale = lax.rsqrt(jnp.transpose(total) / FULL + epsilon)
    q_scale, k_scale = scale[:, 0:1], scale[:, 1:2]
    for h in range(HEADS):
        k_norm = k_in[:, cut(h)].astype(jnp.float32) * k_scale * kg[cut(h)].reshape(1, HEAD_DIM)
        zbuf[1, z, h] = k_norm.astype(jnp.bfloat16)
    for h in range(HEADS):
        column(0, 1, h)
    for h in range(HEADS):
        qn[h] = (q_in[:, cut(h)].astype(jnp.float32) * q_scale * qg[cut(h)].reshape(1, HEAD_DIM)).astype(jnp.bfloat16)
    q_out = pltpu.make_async_copy(qn, qn_o, os.at[0])
    q_out.start()
    order = [(s, t) for s in range(SIDE) for t in range(2)]
    for r in range(1, len(order)):
        s, t = order[r]
        choose(s, t)
        sent(*order[r - 1], 0).wait()
        beside = order[r + 1] if r + 1 < len(order) else None
        if beside is not None:
            arrive(*beside)
        post(s, t, 0, beside if beside is not None and beside[0] < SIDE - 1 else None)
        if r >= len(order) - 3 and r < len(order) - 1:
            cross(r - (len(order) - 3))
        if r == len(order) - 1:
            deliver(0)
        sent(*order[r - 1], 1).wait()
        post(s, t, 1)
    deliver(1)

    def near_rows(t, h):
        return jnp.concatenate(
            [zbuf[t, jnp.maximum(z - 1, 0), h], zbuf[t, z, h], zbuf[t, jnp.minimum(z + 1, SIDE - 1), h]], axis=0)

    place = lax.broadcasted_iota(jnp.int32, (1, NEARK), 1) // TOK
    near_ok = jnp.logical_and(
        jnp.logical_or(place > 0, z > 0), jnp.logical_or(place < 2, z < SIDE - 1))
    half_lane = lax.broadcasted_iota(jnp.int32, (ROWS, HEAD_DIM), 1) < BLOCK

    def near_tile(n, carry):
        h, i = n // (TOK // ROWS), n % (TOK // ROWS)
        rows = pl.ds(i * ROWS, ROWS)
        score = lax.dot_general(qn[h, rows], near_rows(1, h), DIMS, preferred_element_type=jnp.float32)
        score = jnp.where(near_ok, score, masked)
        peak = score.max(-1, keepdims=True)
        prob = jnp.exp2((score - peak) * RATE)
        total = prob.sum(-1, keepdims=True)
        acc[h, rows] = jnp.dot(
            prob.astype(jnp.bfloat16), near_rows(0, h), preferred_element_type=jnp.float32)
        stat[h, rows] = jnp.where(half_lane, peak, total)
        return carry

    lax.fori_loop(0, HEADS * (TOK // ROWS), near_tile, 0)

    def cross_tile(n, carry):
        h, i = n // (TOK // ROWS), n % (TOK // ROWS)
        rows = pl.ds(i * ROWS, ROWS)
        score = lax.dot_general(qn[h, rows], nbuf[1, h], DIMS, preferred_element_type=jnp.float32)
        old_peak, old_total = stat[h, rows][:, 0:1], stat[h, rows][:, BLOCK:BLOCK + 1]
        peak = jnp.maximum(old_peak, score.max(-1, keepdims=True))
        prob = jnp.exp2((score - peak) * RATE)
        shrink = jnp.exp2((old_peak - peak) * RATE)
        total = old_total * shrink + prob.sum(-1, keepdims=True)
        acc[h, rows] = acc[h, rows] * shrink + jnp.dot(
            prob.astype(jnp.bfloat16), nbuf[0, h], preferred_element_type=jnp.float32)
        stat[h, rows] = jnp.where(half_lane, peak, total)
        return carry

    @pl.when(jnp.logical_or(from_prev, from_next))
    def _():
        for t in range(2):
            pltpu.make_async_copy(nbuf.at[t], nbuf.at[t], nr.at[t]).wait()
        lax.fori_loop(0, HEADS * (TOK // ROWS), cross_tile, 0)

    near_out = [pltpu.make_async_copy(acc, acc_o, os.at[1]), pltpu.make_async_copy(stat, stat_o, os.at[2])]
    for c in near_out:
        c.start()

    for t in range(2):
        for s in range(SIDE):
            pltpu.make_async_copy(own.at[t, 0], far_o.at[t, 0], ls.at[s, t]).wait()
            pltpu.make_async_copy(out.at[s, t], out.at[s, t], fr.at[s, t]).wait()

            @pl.when(jnp.logical_and(z - s >= 0, z < SIDE - 1))
            def _():
                z_copy(t, z - s, s, True).wait_send()

            @pl.when(jnp.logical_and(z + s < SIDE, z > 0))
            def _():
                z_copy(t, z + s, s, False).wait_send()

        for way in (0, 1):
            @pl.when(over[way])
            def _():
                near_copy(t, way).wait_send()

            @pl.when(jnp.logical_and(over[way], z != goal[way]))
            def _():
                last_copy(t, way).wait_send()
    sent(*order[-1], 0).wait()
    sent(*order[-1], 1).wait()
    q_out.wait()
    for c in near_out:
        c.wait()


def spread(query, key, value, q_gain, k_gain, far_pick):
    vmem = pl.BlockSpec(memory_space=pltpu.VMEM)
    hbm = pl.BlockSpec(memory_space=pl.ANY)
    dma = pltpu.SemaphoreType.DMA
    bf, f32 = jnp.bfloat16, jnp.float32
    heads = (HEADS, TOK, HEAD_DIM)
    return pl.pallas_call(
        spread_kernel,
        out_shape=(
            jax.ShapeDtypeStruct(heads, bf),
            jax.ShapeDtypeStruct(heads, f32),
            jax.ShapeDtypeStruct(heads, f32),
            jax.ShapeDtypeStruct((2, FRAMES, HEADS, BLOCK, HEAD_DIM), bf),
        ),
        in_specs=[hbm] * 3 + [vmem] * 2 + [pl.BlockSpec(memory_space=pltpu.SMEM)],
        out_specs=(hbm,) * 4,
        scratch_shapes=[
            pltpu.VMEM((TOK, WIDTH), bf),
            pltpu.VMEM((TOK, WIDTH), bf),
            pltpu.VMEM(heads, bf),
            pltpu.VMEM(heads, f32),
            pltpu.VMEM(heads, f32),
            pltpu.VMEM((2, SIDE) + heads, bf),
            pltpu.VMEM((SIDE, 2, PEERS, HEADS, BLOCK, HEAD_DIM), bf),
            pltpu.VMEM((2, SIDE, HEADS, BLOCK, HEAD_DIM), bf),
            pltpu.VMEM((2, 2, HEADS, 2 * BLOCK, HEAD_DIM), bf),
            pltpu.VMEM((2,) + heads, bf),
            pltpu.VMEM((8, TOK), f32),
            pltpu.VMEM((GROUPS, 8, TOK), f32),
            dma((2 + HEADS,)),
            dma((2, SIDE, 2)), dma((SIDE, 2)),
            dma((SIDE, 2, 2)), dma((SIDE, 2)),
            dma((2, 2)), dma((2, 2)), dma((2, 2)), dma((2,)),
            dma((GROUPS,)), dma((GROUPS,)),
            dma((SIDE, 2)), dma((3,)),
        ],
        compiler_params=pltpu.CompilerParams(
            collective_id=0, has_side_effects=True, vmem_limit_bytes=60 << 20),
    )(query, key, value, q_gain, k_gain, far_pick)


def attend_kernel(lists, q, acc, stat, far, o):
    slot = lax.broadcasted_iota(jnp.int32, (1, FARK), 1) // BLOCK
    scores, picked = [], []
    for b in range(BLOCKS):
        sources = [lists[b * NFAR + s] for s in SLOTS]
        bias = jnp.zeros((1, FARK), jnp.float32)
        for i, g in enumerate(sources):
            bias = jnp.where(slot == i, jnp.where(g >= 0, 0.0, masked), bias)
        held = [jnp.maximum(g, 0) for g in sources]
        far_k = jnp.concatenate([far[1, g, 0] for g in held], axis=0)
        picked.append(held)
        scores.append(lax.dot_general(
            q[0, b * BLOCK:(b + 1) * BLOCK], far_k, DIMS, preferred_element_type=jnp.float32) + bias)
    for b in range(BLOCKS):
        rows = slice(b * BLOCK, (b + 1) * BLOCK)
        near_peak, near_total = stat[0, rows, 0:1], stat[0, rows, BLOCK:BLOCK + 1]
        peak = jnp.maximum(near_peak, scores[b].max(-1, keepdims=True))
        prob = jnp.exp2((scores[b] - peak) * RATE)
        shrink = jnp.exp2((near_peak - peak) * RATE)
        total = near_total * shrink + prob.sum(-1, keepdims=True)
        far_v = jnp.concatenate([far[0, g, 0] for g in picked[b]], axis=0)
        sums = acc[0, rows] * shrink + jnp.dot(
            prob.astype(jnp.bfloat16), far_v, preferred_element_type=jnp.float32)
        o[rows] = (sums / total).astype(jnp.bfloat16)


def attend(lists, q, acc, stat, far):
    head = pl.BlockSpec((1, TOK, HEAD_DIM), lambda h, _: (h, 0, 0))
    return pl.pallas_call(
        attend_kernel,
        out_shape=jax.ShapeDtypeStruct((TOK, WIDTH), jnp.bfloat16),
        grid_spec=pltpu.PrefetchScalarGridSpec(
            num_scalar_prefetch=1,
            grid=(HEADS,),
            in_specs=[head] * 3 + [
                pl.BlockSpec((2, FRAMES, 1, BLOCK, HEAD_DIM), lambda h, _: (0, 0, h, 0, 0)),
            ],
            out_specs=pl.BlockSpec((TOK, HEAD_DIM), lambda h, _: (0, h)),
        ),
        compiler_params=pltpu.CompilerParams(vmem_limit_bytes=60 << 20),
    )(lists, q, acc, stat, far)


def local(query, key, value, q_gain, k_gain, far_frames, far_pick):
    frame = lax.axis_index("tm")
    mine = lax.dynamic_slice_in_dim(far_frames, frame * BLOCKS, BLOCKS, 0)
    held = spread(
        query, key, value, q_gain, k_gain, far_pick)
    return attend(mine.reshape(-1), *held)


def solution(mesh):
    placed = (P("tm", "head"), P("tm", "head"), P("tm", "head"), P("head"), P("head"), P(), P())
    return jax.shard_map(
        local, mesh=mesh, in_specs=placed, out_specs=P("tm", "head"), check_vma=False
    )
```

```python
import functools

import jax
import jax.numpy as jnp
from jax import lax
from jax.experimental import pallas as pl
from jax.experimental.pallas import tpu as pltpu
from jax.sharding import PartitionSpec as P

HEAD_DIM = 128
BLOCK = 64
NFAR = 12
SIDE = 4
HEADS = 5
BLOCKS = 8
FRAMES = 64
GROUPS = 8
TOK = BLOCK * BLOCKS
WIDTH = HEADS * HEAD_DIM
FULL = WIDTH * GROUPS
SLOTS = (0, 1, 2, 3, 4, 6, 7, 8, 9, 10)
FARK = len(SLOTS) * BLOCK
NEARK = 3 * TOK
epsilon = 1e-06
masked = -1e30
MESH = pl.DeviceIdType.MESH
PLANE = (
    (2, 2), (1, 1), (3, 3), (1, 3), (3, 1), (2, 1), (1, 2), (2, 3),
    (3, 2), (2, 0), (0, 2), (1, 0), (0, 1), (3, 0), (0, 3),
)
PEERS = len(PLANE)
HALF = 8
ROWS = 256
RATE = HEAD_DIM ** (-0.5) * 1.4426950408889634
DIMS = (((1,), (1,)), ((), ()))


def spread_kernel(
    q, k, v, qg, kg, pick, lists, o,
    q_in, k_in, qn, acc, stat, zbuf, out, own, stage, nbuf, sums, parts, far_v, far_k, weight, far_stat, o_heads,
    ins, zs, zr, fs, fr, ns, yr, cs, nr, hs, hr, ls, os,
):
    far = (far_v, far_k)
    frame = lax.axis_index("tm")
    group = lax.axis_index("head")
    col, z = frame // SIDE, frame % SIDE
    x, y = col // SIDE, col % SIDE

    def tm(dev):
        return {"tm": dev}

    def plane_peer(d):
        return (((x + d[0]) % SIDE) * SIDE + (y + d[1]) % SIDE) * SIDE + z

    def cut(h):
        return slice(h * HEAD_DIM, (h + 1) * HEAD_DIM)

    has_next, has_prev = col < 15, col > 0
    from_prev = jnp.logical_and(z == 0, has_prev)
    from_next = jnp.logical_and(z == SIDE - 1, has_next)

    loads = [pltpu.make_async_copy(q, q_in, ins.at[0]), pltpu.make_async_copy(k, k_in, ins.at[1])]
    loads += [pltpu.make_async_copy(v.at[:, cut(h)], zbuf.at[0, z, h], ins.at[2 + h]) for h in range(HEADS)]
    for c in loads:
        c.start()

    barrier = pltpu.get_barrier_semaphore()

    def greet(dev):
        pl.semaphore_signal(barrier, inc=1, device_id=dev, device_id_type=MESH)

    for d in PLANE:
        greet(tm(plane_peer(d)))
    for j in range(1, GROUPS):
        greet({"head": (group + j) % GROUPS})

    for j in range(1, SIDE):
        greet(tm(col * SIDE + (z + j) % SIDE))

    loads[0].wait()
    loads[1].wait()
    lane = lax.broadcasted_iota(jnp.int32, (TOK, HEAD_DIM), 1)
    q_part = jnp.sum(jnp.square(q_in[...].astype(jnp.float32)), axis=1, keepdims=True)
    k_part = jnp.sum(jnp.square(k_in[...].astype(jnp.float32)), axis=1, keepdims=True)
    both = jnp.where(lane == 0, q_part, jnp.where(lane == 1, k_part, 0.0))
    sums[...] = jnp.transpose(both)[:8]

    for c in loads[2:]:
        c.wait()
    pl.semaphore_wait(barrier, PEERS + GROUPS - 1 + SIDE - 1)

    sum_copies = []
    for j in range(1, GROUPS):
        c = pltpu.make_async_remote_copy(
            sums, parts.at[j], hs.at[j], hr.at[j],
            device_id={"head": (group + j) % GROUPS}, device_id_type=MESH)
        c.start()
        sum_copies.append(c)

    def z_copy(t, j, hop, right, h=None):
        dev = frame + 1 if right else frame - 1
        part = zbuf.at[t, j] if h is None else zbuf.at[t, j, h]
        return pltpu.make_async_remote_copy(
            part, part, zs.at[int(right), hop, t], zr.at[j, t],
            device_id=tm(dev), device_id_type=MESH)

    quarter = pl.ds(2 * BLOCK * z, 2 * BLOCK)
    over = (has_prev, has_next)
    goal = (0, SIDE - 1)

    def near_copy(t, up, h=None):
        heads = slice(None) if h is None else h
        return pltpu.make_async_remote_copy(
            zbuf.at[t, SIDE - 1 if up else 0, heads, quarter], stage.at[1 - up, t, heads],
            ns.at[up, t], yr.at[1 - up, t],
            device_id=tm(frame + SIDE if up else frame - SIDE), device_id_type=MESH)

    def cross(t):
        for h in range(HEADS):
            for up in (1, 0):
                @pl.when(over[up])
                def _():
                    near_copy(t, up, h).start()

    def last_copy(t, way):
        return pltpu.make_async_remote_copy(
            stage.at[way, t], nbuf.at[t, :, quarter], cs.at[way, t], nr.at[t],
            device_id=tm(col * SIDE + goal[way]), device_id_type=MESH)

    def deliver(t):
        for way in (0, 1):
            @pl.when(over[way])
            def _():
                pltpu.make_async_copy(stage.at[way, t], stage.at[way, t], yr.at[way, t]).wait()

                @pl.when(z != goal[way])
                def _():
                    last_copy(t, way).start()

                @pl.when(z == goal[way])
                def _():
                    pltpu.make_async_copy(stage.at[way, t], nbuf.at[t, :, quarter], nr.at[t]).start()

    def step_frame(s):
        if s == 0:
            return z
        if s == SIDE - 1:
            return jnp.where(z < 2, SIDE - 1, 0)
        table = {1: (1, 0, 3, 2), 2: (2, 2, 1, 1)}[s]
        r = jnp.int32(table[0])
        for i in range(1, SIDE):
            r = jnp.where(z == i, table[i], r)
        return r

    def far_copy(s, t, i, j):
        return pltpu.make_async_remote_copy(
            out.at[s, t, i], far[t].at[col * SIDE + j], fs.at[s, t, i // HALF], fr.at[s, t],
            device_id=tm(plane_peer(PLANE[i])), device_id_type=MESH)

    def sent(s, t, half):
        part = out.at[s, t, pl.ds(half * HALF, HALF if half == 0 else PEERS - HALF)]
        return pltpu.make_async_copy(part, part, fs.at[s, t, half])

    def arrive(s, t):
        @pl.when(z - s >= 0)
        def _():
            z_copy(t, z - s, s, True).wait_recv()

        @pl.when(z + s < SIDE)
        def _():
            z_copy(t, z + s, s, False).wait_recv()

    def column(s, t, h):
        @pl.when(jnp.logical_and(z - s >= 0, z < SIDE - 1))
        def _():
            z_copy(t, z - s, s, True, h).start()

        @pl.when(jnp.logical_and(z + s < SIDE, z > 0))
        def _():
            z_copy(t, z + s, s, False, h).start()

    def choose(s, t):
        j = step_frame(s)
        g = col * SIDE + j
        picks = [pick[plane_peer(d), g] for d in PLANE] + [pick[frame, g]]

        def one_head(h, carry):
            blocks = [zbuf[t, j, h, b * BLOCK:(b + 1) * BLOCK] for b in range(BLOCKS)]
            for i, p in enumerate(picks):
                level = blocks
                for bit in range(3):
                    odd = ((p // (1 << bit)) % 2) == 1
                    level = [jnp.where(odd, level[2 * m + 1], level[2 * m]) for m in range(len(level) // 2)]
                if i < PEERS:
                    out[s, t, i, h] = level[0]
                else:
                    own[t, j, h] = level[0]
            return carry

        lax.fori_loop(0, HEADS, one_head, 0)
        pltpu.make_async_copy(own.at[t, j], far[t].at[g], ls.at[s, t]).start()

    def post(s, t, half, beside=None):
        j = step_frame(s)
        for i in range(PEERS):
            if i // HALF == half:
                far_copy(s, t, i, j).start()
                if beside is not None and i % HALF < HEADS:
                    column(*beside, i % HALF)

    for h in range(HEADS):
        column(0, 0, h)
    choose(0, 0)
    post(0, 0, 0)
    post(0, 0, 1)
    for c in sum_copies:
        c.wait()
    total = sums[...]
    for j in range(1, GROUPS):
        total = total + parts[j]
    total = jnp.concatenate([total, jnp.zeros((HEAD_DIM - 8, TOK), jnp.float32)], axis=0)
    scale = lax.rsqrt(jnp.transpose(total) / FULL + epsilon)
    q_scale, k_scale = scale[:, 0:1], scale[:, 1:2]
    for h in range(HEADS):
        k_norm = k_in[:, cut(h)].astype(jnp.float32) * k_scale * kg[cut(h)].reshape(1, HEAD_DIM)
        zbuf[1, z, h] = k_norm.astype(jnp.bfloat16)
    for h in range(HEADS):
        column(0, 1, h)
    for h in range(HEADS):
        qn[h] = (q_in[:, cut(h)].astype(jnp.float32) * q_scale * qg[cut(h)].reshape(1, HEAD_DIM)).astype(jnp.bfloat16)
    order = [(0, 0), (0, 1), (1, 0), (1, 1), (2, 1), (2, 0), (3, 1), (3, 0)]
    for r in range(1, len(order)):
        s, t = order[r]
        beside = order[r + 1] if r + 1 < len(order) else None
        moves = beside is not None and beside[0] < SIDE - 1
        early = beside != (2, 1)
        choose(s, t)
        sent(*order[r - 1], 0).wait()
        if beside is not None and early:
            arrive(*beside)
        post(s, t, 0, beside if moves and early else None)
        if beside is not None and not early:
            arrive(*beside)
        if r == 5:
            cross(1)
        if r == 6:
            cross(0)
        if r == 7:
            deliver(1)
        sent(*order[r - 1], 1).wait()
        post(s, t, 1, beside if moves and not early else None)
    deliver(0)

    def near_rows(t, h):
        return jnp.concatenate(
            [zbuf[t, jnp.maximum(z - 1, 0), h], zbuf[t, z, h], zbuf[t, jnp.minimum(z + 1, SIDE - 1), h]], axis=0)

    place = lax.broadcasted_iota(jnp.int32, (1, NEARK), 1) // TOK
    near_ok = jnp.logical_and(
        jnp.logical_or(place > 0, z > 0), jnp.logical_or(place < 2, z < SIDE - 1))
    half_lane = lax.broadcasted_iota(jnp.int32, (ROWS, HEAD_DIM), 1) < BLOCK

    def near_tile(n, carry):
        h, i = n // (TOK // ROWS), n % (TOK // ROWS)
        rows = pl.ds(i * ROWS, ROWS)
        score = lax.dot_general(qn[h, rows], near_rows(1, h), DIMS, preferred_element_type=jnp.float32)
        score = jnp.where(near_ok, score, masked)
        peak = score.max(-1, keepdims=True)
        prob = jnp.exp2((score - peak) * RATE)
        total = prob.sum(-1, keepdims=True)
        acc[h, rows] = jnp.dot(
            prob.astype(jnp.bfloat16), near_rows(0, h), preferred_element_type=jnp.float32)
        stat[h, rows] = jnp.where(half_lane, peak, total)
        return carry

    lax.fori_loop(0, HEADS * (TOK // ROWS), near_tile, 0)

    def arrived(t):
        for s in range(SIDE):
            pltpu.make_async_copy(own.at[t, 0], far[t].at[0], ls.at[s, t]).wait()
            pltpu.make_async_copy(out.at[s, t], out.at[s, t], fr.at[s, t]).wait()

    slot = lax.broadcasted_iota(jnp.int32, (1, FARK), 1) // BLOCK

    def far_scores(h, carry):
        scores = []
        for b in range(BLOCKS):
            sources = [lists[b * NFAR + n] for n in SLOTS]
            bias = jnp.zeros((1, FARK), jnp.float32)
            for n, g in enumerate(sources):
                bias = jnp.where(slot == n, jnp.where(g >= 0, 0.0, masked), bias)
            keys = jnp.concatenate([far_k[jnp.maximum(g, 0), h] for g in sources], axis=0)
            scores.append(lax.dot_general(
                qn[h, b * BLOCK:(b + 1) * BLOCK], keys, DIMS, preferred_element_type=jnp.float32) + bias)
        for b in range(BLOCKS):
            peak = scores[b].max(-1, keepdims=True)
            prob = jnp.exp2((scores[b] - peak) * RATE)
            weight[h, b] = prob.astype(jnp.bfloat16)
            far_stat[h, b * BLOCK:(b + 1) * BLOCK] = jnp.where(
                half_lane[:BLOCK], peak, prob.sum(-1, keepdims=True))
        return carry

    arrived(1)
    lax.fori_loop(0, HEADS, far_scores, 0)

    def cross_tile(n, carry):
        h, i = n // (TOK // ROWS), n % (TOK // ROWS)
        rows = pl.ds(i * ROWS, ROWS)
        score = lax.dot_general(qn[h, rows], nbuf[1, h], DIMS, preferred_element_type=jnp.float32)
        old_peak, old_total = stat[h, rows][:, 0:1], stat[h, rows][:, BLOCK:BLOCK + 1]
        peak = jnp.maximum(old_peak, score.max(-1, keepdims=True))
        prob = jnp.exp2((score - peak) * RATE)
        shrink = jnp.exp2((old_peak - peak) * RATE)
        total = old_total * shrink + prob.sum(-1, keepdims=True)
        acc[h, rows] = acc[h, rows] * shrink + jnp.dot(
            prob.astype(jnp.bfloat16), nbuf[0, h], preferred_element_type=jnp.float32)
        stat[h, rows] = jnp.where(half_lane, peak, total)
        return carry

    @pl.when(jnp.logical_or(from_prev, from_next))
    def _():
        for t in range(2):
            pltpu.make_async_copy(nbuf.at[t], nbuf.at[t], nr.at[t]).wait()
        lax.fori_loop(0, HEADS * (TOK // ROWS), cross_tile, 0)

    def o_copy(h):
        cols = pl.ds(pl.multiple_of(h * HEAD_DIM, HEAD_DIM), HEAD_DIM)
        return pltpu.make_async_copy(o_heads.at[h], o.at[:, cols], os.at[h])

    def far_values(h, carry):
        for b in range(BLOCKS):
            rows = slice(b * BLOCK, (b + 1) * BLOCK)
            vals = jnp.concatenate(
                [far_v[jnp.maximum(lists[b * NFAR + n], 0), h] for n in SLOTS], axis=0)
            near_peak, near_total = stat[h, rows][:, 0:1], stat[h, rows][:, BLOCK:BLOCK + 1]
            far_peak, far_total = far_stat[h, rows][:, 0:1], far_stat[h, rows][:, BLOCK:BLOCK + 1]
            peak = jnp.maximum(near_peak, far_peak)
            a = jnp.exp2((near_peak - peak) * RATE)
            c = jnp.exp2((far_peak - peak) * RATE)
            mixed = acc[h, rows] * a + jnp.dot(weight[h, b], vals, preferred_element_type=jnp.float32) * c
            o_heads[h, rows] = (mixed / (near_total * a + far_total * c)).astype(jnp.bfloat16)
        o_copy(h).start()
        return carry

    arrived(0)
    lax.fori_loop(0, HEADS, far_values, 0)

    for t in range(2):
        for s in range(SIDE):
            @pl.when(jnp.logical_and(z - s >= 0, z < SIDE - 1))
            def _():
                z_copy(t, z - s, s, True).wait_send()

            @pl.when(jnp.logical_and(z + s < SIDE, z > 0))
            def _():
                z_copy(t, z + s, s, False).wait_send()

        for way in (0, 1):
            @pl.when(over[way])
            def _():
                near_copy(t, way).wait_send()

            @pl.when(jnp.logical_and(over[way], z != goal[way]))
            def _():
                last_copy(t, way).wait_send()
    sent(*order[-1], 0).wait()
    sent(*order[-1], 1).wait()
    for h in range(HEADS):
        o_copy(h).wait()


def spread(query, key, value, q_gain, k_gain, far_pick, lists):
    vmem = pl.BlockSpec(memory_space=pltpu.VMEM)
    hbm = pl.BlockSpec(memory_space=pl.ANY)
    smem = pl.BlockSpec(memory_space=pltpu.SMEM)
    dma = pltpu.SemaphoreType.DMA
    bf, f32 = jnp.bfloat16, jnp.float32
    heads = (HEADS, TOK, HEAD_DIM)
    far = (FRAMES, HEADS, BLOCK, HEAD_DIM)
    return pl.pallas_call(
        spread_kernel,
        out_shape=jax.ShapeDtypeStruct((TOK, WIDTH), bf),
        in_specs=[hbm] * 3 + [vmem] * 2 + [smem] * 2,
        out_specs=hbm,
        scratch_shapes=[
            pltpu.VMEM((TOK, WIDTH), bf),
            pltpu.VMEM((TOK, WIDTH), bf),
            pltpu.VMEM(heads, bf),
            pltpu.VMEM(heads, f32),
            pltpu.VMEM(heads, f32),
            pltpu.VMEM((2, SIDE) + heads, bf),
            pltpu.VMEM((SIDE, 2, PEERS, HEADS, BLOCK, HEAD_DIM), bf),
            pltpu.VMEM((2, SIDE, HEADS, BLOCK, HEAD_DIM), bf),
            pltpu.VMEM((2, 2, HEADS, 2 * BLOCK, HEAD_DIM), bf),
            pltpu.VMEM((2,) + heads, bf),
            pltpu.VMEM((8, TOK), f32),
            pltpu.VMEM((GROUPS, 8, TOK), f32),
            pltpu.VMEM(far, bf),
            pltpu.VMEM(far, bf),
            pltpu.VMEM((HEADS, BLOCKS, BLOCK, FARK), bf),
            pltpu.VMEM(heads, f32),
            pltpu.VMEM(heads, bf),
            dma((2 + HEADS,)),
            dma((2, SIDE, 2)), dma((SIDE, 2)),
            dma((SIDE, 2, 2)), dma((SIDE, 2)),
            dma((2, 2)), dma((2, 2)), dma((2, 2)), dma((2,)),
            dma((GROUPS,)), dma((GROUPS,)),
            dma((SIDE, 2)), dma((HEADS,)),
        ],
        compiler_params=pltpu.CompilerParams(
            collective_id=0, has_side_effects=True, vmem_limit_bytes=60 << 20),
    )(query, key, value, q_gain, k_gain, far_pick, lists)


def local(query, key, value, q_gain, k_gain, far_frames, far_pick):
    frame = lax.axis_index("tm")
    mine = lax.dynamic_slice_in_dim(far_frames, frame * BLOCKS, BLOCKS, 0)
    return spread(query, key, value, q_gain, k_gain, far_pick, mine.reshape(-1))


def solution(mesh):
    placed = (P("tm", "head"), P("tm", "head"), P("tm", "head"), P("head"), P("head"), P(), P())
    return jax.shard_map(
        local, mesh=mesh, in_specs=placed, out_specs=P("tm", "head"), check_vma=False
    )
```

```python
import functools

import jax
import jax.numpy as jnp
from jax import lax
from jax.experimental import pallas as pl
from jax.experimental.pallas import tpu as pltpu
from jax.sharding import PartitionSpec as P

HEAD_DIM = 128
BLOCK = 64
NFAR = 12
SIDE = 4
HEADS = 5
BLOCKS = 8
FRAMES = 64
GROUPS = 8
TOK = BLOCK * BLOCKS
WIDTH = HEADS * HEAD_DIM
FULL = WIDTH * GROUPS
SLOTS = (0, 1, 2, 3, 4, 6, 7, 8, 9, 10)
FARK = len(SLOTS) * BLOCK
NEARK = 3 * TOK
epsilon = 1e-06
masked = -1e30
MESH = pl.DeviceIdType.MESH
PLANE = (
    (2, 2), (2, 1), (1, 2), (2, 3), (3, 2), (1, 1), (3, 3), (1, 3),
    (3, 1), (2, 0), (0, 2), (1, 0), (0, 1), (3, 0), (0, 3),
)
PEERS = len(PLANE)
HALF = 8
ROWS = 256
RATE = HEAD_DIM ** (-0.5) * 1.4426950408889634
DIMS = (((1,), (1,)), ((), ()))


def spread_kernel(
    q, k, v, qg, kg, pick, lists, o,
    q_in, k_in, qn, acc, stat, zbuf, out, own, stage, nbuf, sums, parts, far_v, far_k, weight, far_stat, o_heads,
    ins, zs, zr, fs, fr, ns, yr, cs, nr, hs, hr, ls, os,
):
    far = (far_v, far_k)
    frame = lax.axis_index("tm")
    group = lax.axis_index("head")
    col, z = frame // SIDE, frame % SIDE
    x, y = col // SIDE, col % SIDE

    def tm(dev):
        return {"tm": dev}

    def plane_peer(d):
        return (((x + d[0]) % SIDE) * SIDE + (y + d[1]) % SIDE) * SIDE + z

    def cut(h):
        return slice(h * HEAD_DIM, (h + 1) * HEAD_DIM)

    has_next, has_prev = col < 15, col > 0
    from_prev = jnp.logical_and(z == 0, has_prev)
    from_next = jnp.logical_and(z == SIDE - 1, has_next)

    loads = [pltpu.make_async_copy(q, q_in, ins.at[0]), pltpu.make_async_copy(k, k_in, ins.at[1])]
    loads += [pltpu.make_async_copy(v.at[:, cut(h)], zbuf.at[0, z, h], ins.at[2 + h]) for h in range(HEADS)]
    for c in loads:
        c.start()

    barrier = pltpu.get_barrier_semaphore()

    def greet(dev):
        pl.semaphore_signal(barrier, inc=1, device_id=dev, device_id_type=MESH)

    for d in PLANE:
        greet(tm(plane_peer(d)))
    for j in range(1, GROUPS):
        greet({"head": (group + j) % GROUPS})

    for j in range(1, SIDE):
        greet(tm(col * SIDE + (z + j) % SIDE))

    loads[0].wait()
    loads[1].wait()
    lane = lax.broadcasted_iota(jnp.int32, (TOK, HEAD_DIM), 1)
    q_part = jnp.sum(jnp.square(q_in[...].astype(jnp.float32)), axis=1, keepdims=True)
    k_part = jnp.sum(jnp.square(k_in[...].astype(jnp.float32)), axis=1, keepdims=True)
    both = jnp.where(lane == 0, q_part, jnp.where(lane == 1, k_part, 0.0))
    sums[...] = jnp.transpose(both)[:8]

    for c in loads[2:]:
        c.wait()
    pl.semaphore_wait(barrier, PEERS + GROUPS - 1 + SIDE - 1)

    sum_copies = []
    for j in range(1, GROUPS):
        c = pltpu.make_async_remote_copy(
            sums, parts.at[j], hs.at[j], hr.at[j],
            device_id={"head": (group + j) % GROUPS}, device_id_type=MESH)
        c.start()
        sum_copies.append(c)

    def z_copy(t, j, hop, right, h=None):
        dev = frame + 1 if right else frame - 1
        part = zbuf.at[t, j] if h is None else zbuf.at[t, j, h]
        return pltpu.make_async_remote_copy(
            part, part, zs.at[int(right), hop, t], zr.at[j, t],
            device_id=tm(dev), device_id_type=MESH)

    quarter = pl.ds(2 * BLOCK * z, 2 * BLOCK)
    over = (has_prev, has_next)
    goal = (0, SIDE - 1)

    def near_copy(t, up, h=None):
        heads = slice(None) if h is None else h
        return pltpu.make_async_remote_copy(
            zbuf.at[t, SIDE - 1 if up else 0, heads, quarter], stage.at[1 - up, t, heads],
            ns.at[up, t], yr.at[1 - up, t],
            device_id=tm(frame + SIDE if up else frame - SIDE), device_id_type=MESH)

    def cross(t, late):
        for h in range(HEADS):
            for up in (1, 0):
                outer = z == (0 if up else SIDE - 1)

                @pl.when(jnp.logical_and(over[up], outer if late else jnp.logical_not(outer)))
                def _():
                    near_copy(t, up, h).start()

    def last_copy(t, way):
        return pltpu.make_async_remote_copy(
            stage.at[way, t], nbuf.at[t, :, quarter], cs.at[way, t], nr.at[t],
            device_id=tm(col * SIDE + goal[way]), device_id_type=MESH)

    def deliver(t):
        for way in (0, 1):
            @pl.when(over[way])
            def _():
                pltpu.make_async_copy(stage.at[way, t], stage.at[way, t], yr.at[way, t]).wait()

                @pl.when(z != goal[way])
                def _():
                    last_copy(t, way).start()

                @pl.when(z == goal[way])
                def _():
                    pltpu.make_async_copy(stage.at[way, t], nbuf.at[t, :, quarter], nr.at[t]).start()

    def step_frame(s):
        if s == 0:
            return z
        if s == SIDE - 1:
            return jnp.where(z < 2, SIDE - 1, 0)
        table = {1: (1, 0, 3, 2), 2: (2, 2, 1, 1)}[s]
        r = jnp.int32(table[0])
        for i in range(1, SIDE):
            r = jnp.where(z == i, table[i], r)
        return r

    def far_copy(s, t, i, j):
        return pltpu.make_async_remote_copy(
            out.at[s, t, i], far[t].at[col * SIDE + j], fs.at[s, t, i // HALF], fr.at[s, t],
            device_id=tm(plane_peer(PLANE[i])), device_id_type=MESH)

    def sent(s, t, half):
        part = out.at[s, t, pl.ds(half * HALF, HALF if half == 0 else PEERS - HALF)]
        return pltpu.make_async_copy(part, part, fs.at[s, t, half])

    def arrive(s, t):
        @pl.when(z - s >= 0)
        def _():
            z_copy(t, z - s, s, True).wait_recv()

        @pl.when(z + s < SIDE)
        def _():
            z_copy(t, z + s, s, False).wait_recv()

    def column(s, t, h):
        @pl.when(jnp.logical_and(z - s >= 0, z < SIDE - 1))
        def _():
            z_copy(t, z - s, s, True, h).start()

        @pl.when(jnp.logical_and(z + s < SIDE, z > 0))
        def _():
            z_copy(t, z + s, s, False, h).start()

    def choose(s, t):
        j = step_frame(s)
        g = col * SIDE + j
        picks = [pick[plane_peer(d), g] for d in PLANE] + [pick[frame, g]]

        def one_head(h, carry):
            blocks = [zbuf[t, j, h, b * BLOCK:(b + 1) * BLOCK] for b in range(BLOCKS)]
            for i, p in enumerate(picks):
                level = blocks
                for bit in range(3):
                    odd = ((p // (1 << bit)) % 2) == 1
                    level = [jnp.where(odd, level[2 * m + 1], level[2 * m]) for m in range(len(level) // 2)]
                if i < PEERS:
                    out[s, t, i, h] = level[0]
                else:
                    own[t, j, h] = level[0]
            return carry

        lax.fori_loop(0, HEADS, one_head, 0)
        pltpu.make_async_copy(own.at[t, j], far[t].at[g], ls.at[s, t]).start()

    def post(s, t, half, beside=None):
        j = step_frame(s)
        for i in range(PEERS):
            if i // HALF == half:
                far_copy(s, t, i, j).start()
                if beside is not None and i % HALF < HEADS:
                    column(*beside, i % HALF)

    for h in range(HEADS):
        column(0, 0, h)
    choose(0, 0)
    post(0, 0, 0)
    post(0, 0, 1)
    for c in sum_copies:
        c.wait()
    total = sums[...]
    for j in range(1, GROUPS):
        total = total + parts[j]
    total = jnp.concatenate([total, jnp.zeros((HEAD_DIM - 8, TOK), jnp.float32)], axis=0)
    scale = lax.rsqrt(jnp.transpose(total) / FULL + epsilon)
    q_scale, k_scale = scale[:, 0:1], scale[:, 1:2]
    for h in range(HEADS):
        k_norm = k_in[:, cut(h)].astype(jnp.float32) * k_scale * kg[cut(h)].reshape(1, HEAD_DIM)
        zbuf[1, z, h] = k_norm.astype(jnp.bfloat16)
    for h in range(HEADS):
        column(0, 1, h)
    for h in range(HEADS):
        qn[h] = (q_in[:, cut(h)].astype(jnp.float32) * q_scale * qg[cut(h)].reshape(1, HEAD_DIM)).astype(jnp.bfloat16)
    def near_rows(t, h):
        return jnp.concatenate(
            [zbuf[t, jnp.maximum(z - 1, 0), h], zbuf[t, z, h], zbuf[t, jnp.minimum(z + 1, SIDE - 1), h]], axis=0)

    place = lax.broadcasted_iota(jnp.int32, (1, NEARK), 1) // TOK
    near_ok = jnp.logical_and(
        jnp.logical_or(place > 0, z > 0), jnp.logical_or(place < 2, z < SIDE - 1))
    half_lane = lax.broadcasted_iota(jnp.int32, (ROWS, HEAD_DIM), 1) < BLOCK

    def near_tile(n, carry):
        h, i = n // (TOK // ROWS), n % (TOK // ROWS)
        rows = pl.ds(i * ROWS, ROWS)
        score = lax.dot_general(qn[h, rows], near_rows(1, h), DIMS, preferred_element_type=jnp.float32)
        score = jnp.where(near_ok, score, masked)
        peak = score.max(-1, keepdims=True)
        prob = jnp.exp2((score - peak) * RATE)
        total = prob.sum(-1, keepdims=True)
        acc[h, rows] = jnp.dot(
            prob.astype(jnp.bfloat16), near_rows(0, h), preferred_element_type=jnp.float32)
        stat[h, rows] = jnp.where(half_lane, peak, total)
        return carry

    order = [(0, 0), (0, 1), (1, 0), (1, 1), (2, 1), (2, 0), (3, 1), (3, 0)]
    for r in range(1, len(order)):
        s, t = order[r]
        beside = order[r + 1] if r + 1 < len(order) else None
        moves = beside is not None and beside[0] < SIDE - 1
        early = beside != (2, 1)
        choose(s, t)
        if beside is not None and early:
            arrive(*beside)
        post(s, t, 0, beside if moves and early else None)
        if beside is not None and not early:
            arrive(*beside)
        if r == 4:
            cross(1, False)
            cross(0, False)
        if r == 5:
            cross(1, True)
        if r == 6:
            cross(0, True)
        if r == 7:
            deliver(1)
        post(s, t, 1, beside if moves and not early else None)
        if r == 7:
            lax.fori_loop(0, HEADS * (TOK // ROWS), near_tile, 0)
    deliver(0)

    def arrived(t):
        for s in range(SIDE):
            pltpu.make_async_copy(own.at[t, 0], far[t].at[0], ls.at[s, t]).wait()
            pltpu.make_async_copy(out.at[s, t], out.at[s, t], fr.at[s, t]).wait()

    slot = lax.broadcasted_iota(jnp.int32, (1, FARK), 1) // BLOCK

    def far_scores(h, carry):
        scores = []
        for b in range(BLOCKS):
            sources = [lists[b * NFAR + n] for n in SLOTS]
            bias = jnp.zeros((1, FARK), jnp.float32)
            for n, g in enumerate(sources):
                bias = jnp.where(slot == n, jnp.where(g >= 0, 0.0, masked), bias)
            keys = jnp.concatenate([far_k[jnp.maximum(g, 0), h] for g in sources], axis=0)
            scores.append(lax.dot_general(
                qn[h, b * BLOCK:(b + 1) * BLOCK], keys, DIMS, preferred_element_type=jnp.float32) + bias)
        for b in range(BLOCKS):
            peak = scores[b].max(-1, keepdims=True)
            prob = jnp.exp2((scores[b] - peak) * RATE)
            weight[h, b] = prob.astype(jnp.bfloat16)
            far_stat[h, b * BLOCK:(b + 1) * BLOCK] = jnp.where(
                half_lane[:BLOCK], peak, prob.sum(-1, keepdims=True))
        return carry

    arrived(1)
    lax.fori_loop(0, HEADS, far_scores, 0)

    def cross_tile(n, carry):
        h, i = n // (TOK // ROWS), n % (TOK // ROWS)
        rows = pl.ds(i * ROWS, ROWS)
        score = lax.dot_general(qn[h, rows], nbuf[1, h], DIMS, preferred_element_type=jnp.float32)
        old_peak, old_total = stat[h, rows][:, 0:1], stat[h, rows][:, BLOCK:BLOCK + 1]
        peak = jnp.maximum(old_peak, score.max(-1, keepdims=True))
        prob = jnp.exp2((score - peak) * RATE)
        shrink = jnp.exp2((old_peak - peak) * RATE)
        total = old_total * shrink + prob.sum(-1, keepdims=True)
        acc[h, rows] = acc[h, rows] * shrink + jnp.dot(
            prob.astype(jnp.bfloat16), nbuf[0, h], preferred_element_type=jnp.float32)
        stat[h, rows] = jnp.where(half_lane, peak, total)
        return carry

    @pl.when(jnp.logical_or(from_prev, from_next))
    def _():
        for t in range(2):
            pltpu.make_async_copy(nbuf.at[t], nbuf.at[t], nr.at[t]).wait()
        lax.fori_loop(0, HEADS * (TOK // ROWS), cross_tile, 0)

    def o_copy(h):
        cols = pl.ds(pl.multiple_of(h * HEAD_DIM, HEAD_DIM), HEAD_DIM)
        return pltpu.make_async_copy(o_heads.at[h], o.at[:, cols], os.at[h])

    def far_values(h, carry):
        for b in range(BLOCKS):
            rows = slice(b * BLOCK, (b + 1) * BLOCK)
            vals = jnp.concatenate(
                [far_v[jnp.maximum(lists[b * NFAR + n], 0), h] for n in SLOTS], axis=0)
            near_peak, near_total = stat[h, rows][:, 0:1], stat[h, rows][:, BLOCK:BLOCK + 1]
            far_peak, far_total = far_stat[h, rows][:, 0:1], far_stat[h, rows][:, BLOCK:BLOCK + 1]
            peak = jnp.maximum(near_peak, far_peak)
            a = jnp.exp2((near_peak - peak) * RATE)
            c = jnp.exp2((far_peak - peak) * RATE)
            mixed = acc[h, rows] * a + jnp.dot(weight[h, b], vals, preferred_element_type=jnp.float32) * c
            o_heads[h, rows] = (mixed / (near_total * a + far_total * c)).astype(jnp.bfloat16)
        o_copy(h).start()
        return carry

    arrived(0)
    lax.fori_loop(0, HEADS, far_values, 0)

    for t in range(2):
        for s in range(SIDE):
            @pl.when(jnp.logical_and(z - s >= 0, z < SIDE - 1))
            def _():
                z_copy(t, z - s, s, True).wait_send()

            @pl.when(jnp.logical_and(z + s < SIDE, z > 0))
            def _():
                z_copy(t, z + s, s, False).wait_send()

        for way in (0, 1):
            @pl.when(over[way])
            def _():
                near_copy(t, way).wait_send()

            @pl.when(jnp.logical_and(over[way], z != goal[way]))
            def _():
                last_copy(t, way).wait_send()
    for st in order:
        sent(*st, 0).wait()
        sent(*st, 1).wait()
    for h in range(HEADS):
        o_copy(h).wait()


def spread(query, key, value, q_gain, k_gain, far_pick, lists):
    vmem = pl.BlockSpec(memory_space=pltpu.VMEM)
    hbm = pl.BlockSpec(memory_space=pl.ANY)
    smem = pl.BlockSpec(memory_space=pltpu.SMEM)
    dma = pltpu.SemaphoreType.DMA
    bf, f32 = jnp.bfloat16, jnp.float32
    heads = (HEADS, TOK, HEAD_DIM)
    far = (FRAMES, HEADS, BLOCK, HEAD_DIM)
    return pl.pallas_call(
        spread_kernel,
        out_shape=jax.ShapeDtypeStruct((TOK, WIDTH), bf),
        in_specs=[hbm] * 3 + [vmem] * 2 + [smem] * 2,
        out_specs=hbm,
        scratch_shapes=[
            pltpu.VMEM((TOK, WIDTH), bf),
            pltpu.VMEM((TOK, WIDTH), bf),
            pltpu.VMEM(heads, bf),
            pltpu.VMEM(heads, f32),
            pltpu.VMEM(heads, f32),
            pltpu.VMEM((2, SIDE) + heads, bf),
            pltpu.VMEM((SIDE, 2, PEERS, HEADS, BLOCK, HEAD_DIM), bf),
            pltpu.VMEM((2, SIDE, HEADS, BLOCK, HEAD_DIM), bf),
            pltpu.VMEM((2, 2, HEADS, 2 * BLOCK, HEAD_DIM), bf),
            pltpu.VMEM((2,) + heads, bf),
            pltpu.VMEM((8, TOK), f32),
            pltpu.VMEM((GROUPS, 8, TOK), f32),
            pltpu.VMEM(far, bf),
            pltpu.VMEM(far, bf),
            pltpu.VMEM((HEADS, BLOCKS, BLOCK, FARK), bf),
            pltpu.VMEM(heads, f32),
            pltpu.VMEM(heads, bf),
            dma((2 + HEADS,)),
            dma((2, SIDE, 2)), dma((SIDE, 2)),
            dma((SIDE, 2, 2)), dma((SIDE, 2)),
            dma((2, 2)), dma((2, 2)), dma((2, 2)), dma((2,)),
            dma((GROUPS,)), dma((GROUPS,)),
            dma((SIDE, 2)), dma((HEADS,)),
        ],
        compiler_params=pltpu.CompilerParams(
            collective_id=0, has_side_effects=True, vmem_limit_bytes=60 << 20),
    )(query, key, value, q_gain, k_gain, far_pick, lists)


def local(query, key, value, q_gain, k_gain, far_frames, far_pick):
    frame = lax.axis_index("tm")
    mine = lax.dynamic_slice_in_dim(far_frames, frame * BLOCKS, BLOCKS, 0)
    return spread(query, key, value, q_gain, k_gain, far_pick, mine.reshape(-1))


def solution(mesh):
    placed = (P("tm", "head"), P("tm", "head"), P("tm", "head"), P("head"), P("head"), P(), P())
    return jax.shard_map(
        local, mesh=mesh, in_specs=placed, out_specs=P("tm", "head"), check_vma=False
    )
```

```python
import functools

import jax
import jax.numpy as jnp
from jax import lax
from jax.experimental import pallas as pl
from jax.experimental.pallas import tpu as pltpu
from jax.sharding import PartitionSpec as P

HEAD_DIM = 128
BLOCK = 64
NFAR = 12
SIDE = 4
HEADS = 5
BLOCKS = 8
FRAMES = 64
GROUPS = 8
TOK = BLOCK * BLOCKS
WIDTH = HEADS * HEAD_DIM
FULL = WIDTH * GROUPS
SLOTS = (0, 1, 2, 3, 4, 6, 7, 8, 9, 10)
FARK = len(SLOTS) * BLOCK
NEARK = 3 * TOK
epsilon = 1e-06
masked = -1e30
MESH = pl.DeviceIdType.MESH
PLANE = (
    (2, 2), (2, 1), (1, 2), (2, 3), (3, 2), (1, 1), (3, 3), (1, 3),
    (3, 1), (2, 0), (0, 2), (1, 0), (0, 1), (3, 0), (0, 3),
)
PEERS = len(PLANE)
HALF = 8
ROWS = 256
RATE = HEAD_DIM ** (-0.5) * 1.4426950408889634
DIMS = (((1,), (1,)), ((), ()))


def spread_kernel(
    q, k, v, qg, kg, pick, lists, o,
    q_in, k_in, qn, acc, stat, zbuf, out, own, stage, nbuf, sums, parts, far_v, far_k, weight, far_stat, o_heads,
    ins, zs, zr, fs, fr, ns, yr, cs, nr, hs, hr, ls, os,
):
    far = (far_v, far_k)
    frame = lax.axis_index("tm")
    group = lax.axis_index("head")
    col, z = frame // SIDE, frame % SIDE
    x, y = col // SIDE, col % SIDE

    def tm(dev):
        return {"tm": dev}

    def plane_peer(d):
        return (((x + d[0]) % SIDE) * SIDE + (y + d[1]) % SIDE) * SIDE + z

    def cut(h):
        return slice(h * HEAD_DIM, (h + 1) * HEAD_DIM)

    has_next, has_prev = col < 15, col > 0
    from_prev = jnp.logical_and(z == 0, has_prev)
    from_next = jnp.logical_and(z == SIDE - 1, has_next)

    loads = [pltpu.make_async_copy(q, q_in, ins.at[0]), pltpu.make_async_copy(k, k_in, ins.at[1])]
    loads += [pltpu.make_async_copy(v.at[:, cut(h)], zbuf.at[0, z, h], ins.at[2 + h]) for h in range(HEADS)]
    for c in loads:
        c.start()

    barrier = pltpu.get_barrier_semaphore()

    def greet(dev):
        pl.semaphore_signal(barrier, inc=1, device_id=dev, device_id_type=MESH)

    for d in PLANE:
        greet(tm(plane_peer(d)))
    for j in range(1, GROUPS):
        greet({"head": (group + j) % GROUPS})

    for j in range(1, SIDE):
        greet(tm(col * SIDE + (z + j) % SIDE))

    loads[0].wait()
    loads[1].wait()
    lane = lax.broadcasted_iota(jnp.int32, (TOK, HEAD_DIM), 1)
    q_part = jnp.sum(jnp.square(q_in[...].astype(jnp.float32)), axis=1, keepdims=True)
    k_part = jnp.sum(jnp.square(k_in[...].astype(jnp.float32)), axis=1, keepdims=True)
    both = jnp.where(lane == 0, q_part, jnp.where(lane == 1, k_part, 0.0))
    sums[...] = jnp.transpose(both)[:8]

    for c in loads[2:]:
        c.wait()
    pl.semaphore_wait(barrier, PEERS + GROUPS - 1 + SIDE - 1)

    sum_copies = []
    for j in range(1, GROUPS):
        c = pltpu.make_async_remote_copy(
            sums, parts.at[j], hs.at[j], hr.at[j],
            device_id={"head": (group + j) % GROUPS}, device_id_type=MESH)
        c.start()
        sum_copies.append(c)

    def z_copy(t, j, hop, right, h=None):
        dev = frame + 1 if right else frame - 1
        part = zbuf.at[t, j] if h is None else zbuf.at[t, j, h]
        return pltpu.make_async_remote_copy(
            part, part, zs.at[int(right), hop, t], zr.at[j, t],
            device_id=tm(dev), device_id_type=MESH)

    quarter = pl.ds(2 * BLOCK * z, 2 * BLOCK)
    over = (has_prev, has_next)
    goal = (0, SIDE - 1)

    def near_copy(t, up, h=None):
        heads = slice(None) if h is None else h
        return pltpu.make_async_remote_copy(
            zbuf.at[t, SIDE - 1 if up else 0, heads, quarter], stage.at[1 - up, t, heads],
            ns.at[up, t], yr.at[1 - up, t],
            device_id=tm(frame + SIDE if up else frame - SIDE), device_id_type=MESH)

    def cross(t, late):
        for h in range(HEADS):
            for up in (1, 0):
                outer = z == (0 if up else SIDE - 1)

                @pl.when(jnp.logical_and(over[up], outer if late else jnp.logical_not(outer)))
                def _():
                    near_copy(t, up, h).start()

    def last_copy(t, way):
        return pltpu.make_async_remote_copy(
            stage.at[way, t], nbuf.at[t, :, quarter], cs.at[way, t], nr.at[t],
            device_id=tm(col * SIDE + goal[way]), device_id_type=MESH)

    def deliver(t):
        for way in (0, 1):
            @pl.when(over[way])
            def _():
                pltpu.make_async_copy(stage.at[way, t], stage.at[way, t], yr.at[way, t]).wait()

                @pl.when(z != goal[way])
                def _():
                    last_copy(t, way).start()

                @pl.when(z == goal[way])
                def _():
                    pltpu.make_async_copy(stage.at[way, t], nbuf.at[t, :, quarter], nr.at[t]).start()

    def step_frame(s):
        if s == 0:
            return z
        if s == SIDE - 1:
            return jnp.where(z < 2, SIDE - 1, 0)
        table = {1: (1, 0, 3, 2), 2: (2, 2, 1, 1)}[s]
        r = jnp.int32(table[0])
        for i in range(1, SIDE):
            r = jnp.where(z == i, table[i], r)
        return r

    def far_copy(s, t, i, j):
        return pltpu.make_async_remote_copy(
            out.at[s, t, i], far[t].at[col * SIDE + j], fs.at[s, t, i // HALF], fr.at[s, t],
            device_id=tm(plane_peer(PLANE[i])), device_id_type=MESH)

    def sent(s, t, half):
        part = out.at[s, t, pl.ds(half * HALF, HALF if half == 0 else PEERS - HALF)]
        return pltpu.make_async_copy(part, part, fs.at[s, t, half])

    def arrive(s, t):
        @pl.when(z - s >= 0)
        def _():
            z_copy(t, z - s, s, True).wait_recv()

        @pl.when(z + s < SIDE)
        def _():
            z_copy(t, z + s, s, False).wait_recv()

    def column(s, t, h):
        @pl.when(jnp.logical_and(z - s >= 0, z < SIDE - 1))
        def _():
            z_copy(t, z - s, s, True, h).start()

        @pl.when(jnp.logical_and(z + s < SIDE, z > 0))
        def _():
            z_copy(t, z + s, s, False, h).start()

    def choose(s, t):
        j = step_frame(s)
        g = col * SIDE + j
        picks = [pick[plane_peer(d), g] for d in PLANE] + [pick[frame, g]]

        def one_head(h, carry):
            blocks = [zbuf[t, j, h, b * BLOCK:(b + 1) * BLOCK] for b in range(BLOCKS)]
            for i, p in enumerate(picks):
                level = blocks
                for bit in range(3):
                    odd = ((p // (1 << bit)) % 2) == 1
                    level = [jnp.where(odd, level[2 * m + 1], level[2 * m]) for m in range(len(level) // 2)]
                if i < PEERS:
                    out[s, t, i, h] = level[0]
                else:
                    own[t, j, h] = level[0]
            return carry

        lax.fori_loop(0, HEADS, one_head, 0)
        pltpu.make_async_copy(own.at[t, j], far[t].at[g], ls.at[s, t]).start()

    def post(s, t, half, beside=None):
        j = step_frame(s)
        for i in range(PEERS):
            if i // HALF == half:
                far_copy(s, t, i, j).start()
                if beside is not None and i % HALF < HEADS:
                    column(*beside, i % HALF)

    for h in range(HEADS):
        column(0, 0, h)
    choose(0, 0)
    post(0, 0, 0)
    post(0, 0, 1)
    for c in sum_copies:
        c.wait()
    total = sums[...]
    for j in range(1, GROUPS):
        total = total + parts[j]
    total = jnp.concatenate([total, jnp.zeros((HEAD_DIM - 8, TOK), jnp.float32)], axis=0)
    scale = lax.rsqrt(jnp.transpose(total) / FULL + epsilon)
    q_scale, k_scale = scale[:, 0:1], scale[:, 1:2]
    for h in range(HEADS):
        k_norm = k_in[:, cut(h)].astype(jnp.float32) * k_scale * kg[cut(h)].reshape(1, HEAD_DIM)
        zbuf[1, z, h] = k_norm.astype(jnp.bfloat16)
    for h in range(HEADS):
        column(0, 1, h)
    for h in range(HEADS):
        qn[h] = (q_in[:, cut(h)].astype(jnp.float32) * q_scale * qg[cut(h)].reshape(1, HEAD_DIM)).astype(jnp.bfloat16)
    def near_rows(t, h):
        return jnp.concatenate(
            [zbuf[t, jnp.maximum(z - 1, 0), h], zbuf[t, z, h], zbuf[t, jnp.minimum(z + 1, SIDE - 1), h]], axis=0)

    place = lax.broadcasted_iota(jnp.int32, (1, NEARK), 1) // TOK
    near_ok = jnp.logical_and(
        jnp.logical_or(place > 0, z > 0), jnp.logical_or(place < 2, z < SIDE - 1))
    half_lane = lax.broadcasted_iota(jnp.int32, (ROWS, HEAD_DIM), 1) < BLOCK

    def near_tile(n, carry):
        h, i = n // (TOK // ROWS), n % (TOK // ROWS)
        rows = pl.ds(i * ROWS, ROWS)
        score = lax.dot_general(qn[h, rows], near_rows(1, h), DIMS, preferred_element_type=jnp.float32)
        score = jnp.where(near_ok, score, masked)
        peak = score.max(-1, keepdims=True)
        prob = jnp.exp2((score - peak) * RATE)
        total = prob.sum(-1, keepdims=True)
        acc[h, rows] = jnp.dot(
            prob.astype(jnp.bfloat16), near_rows(0, h), preferred_element_type=jnp.float32)
        stat[h, rows] = jnp.where(half_lane, peak, total)
        return carry

    order = [(0, 0), (0, 1), (1, 0), (1, 1), (2, 1), (2, 0), (3, 1), (3, 0)]
    for r in range(1, len(order)):
        s, t = order[r]
        beside = order[r + 1] if r + 1 < len(order) else None
        moves = beside is not None and beside[0] < SIDE - 1
        early = beside != (2, 1)
        choose(s, t)
        if beside is not None and early:
            arrive(*beside)
        post(s, t, 0, beside if moves and early else None)
        if beside is not None and not early:
            arrive(*beside)
        if r == 4:
            cross(1, False)
            cross(0, False)
        if r == 5:
            cross(1, True)
        if r == 6:
            cross(0, True)
        if r == 7:
            deliver(1)
        post(s, t, 1, beside if moves and not early else None)
        if r == 7:
            lax.fori_loop(0, HEADS * (TOK // ROWS), near_tile, 0)
    deliver(0)

    def arrived(t):
        for s in range(SIDE):
            pltpu.make_async_copy(own.at[t, 0], far[t].at[0], ls.at[s, t]).wait()
            pltpu.make_async_copy(out.at[s, t], out.at[s, t], fr.at[s, t]).wait()

    slot = lax.broadcasted_iota(jnp.int32, (1, FARK), 1) // BLOCK

    def far_scores(h, carry):
        scores = []
        for b in range(BLOCKS):
            sources = [lists[b * NFAR + n] for n in SLOTS]
            bias = jnp.zeros((1, FARK), jnp.float32)
            for n, g in enumerate(sources):
                bias = jnp.where(slot == n, jnp.where(g >= 0, 0.0, masked), bias)
            keys = jnp.concatenate([far_k[jnp.maximum(g, 0), h] for g in sources], axis=0)
            scores.append(lax.dot_general(
                qn[h, b * BLOCK:(b + 1) * BLOCK], keys, DIMS, preferred_element_type=jnp.float32) + bias)
        for b in range(BLOCKS):
            peak = scores[b].max(-1, keepdims=True)
            prob = jnp.exp2((scores[b] - peak) * RATE)
            weight[h, b] = prob.astype(jnp.bfloat16)
            far_stat[h, b * BLOCK:(b + 1) * BLOCK] = jnp.where(
                half_lane[:BLOCK], peak, prob.sum(-1, keepdims=True))
        return carry

    def cross_tile(n, carry):
        h, i = n // (TOK // ROWS), n % (TOK // ROWS)
        rows = pl.ds(i * ROWS, ROWS)
        score = lax.dot_general(qn[h, rows], nbuf[1, h], DIMS, preferred_element_type=jnp.float32)
        old_peak, old_total = stat[h, rows][:, 0:1], stat[h, rows][:, BLOCK:BLOCK + 1]
        peak = jnp.maximum(old_peak, score.max(-1, keepdims=True))
        prob = jnp.exp2((score - peak) * RATE)
        shrink = jnp.exp2((old_peak - peak) * RATE)
        total = old_total * shrink + prob.sum(-1, keepdims=True)
        acc[h, rows] = acc[h, rows] * shrink + jnp.dot(
            prob.astype(jnp.bfloat16), nbuf[0, h], preferred_element_type=jnp.float32)
        stat[h, rows] = jnp.where(half_lane, peak, total)
        return carry

    @pl.when(jnp.logical_or(from_prev, from_next))
    def _():
        for t in range(2):
            pltpu.make_async_copy(nbuf.at[t], nbuf.at[t], nr.at[t]).wait()
        lax.fori_loop(0, HEADS * (TOK // ROWS), cross_tile, 0)

    arrived(1)
    lax.fori_loop(0, HEADS, far_scores, 0)

    def factors(h, carry):
        near_peak, near_total = stat[h][:, 0:1], stat[h][:, BLOCK:BLOCK + 1]
        far_peak, far_total = far_stat[h][:, 0:1], far_stat[h][:, BLOCK:BLOCK + 1]
        peak = jnp.maximum(near_peak, far_peak)
        a = jnp.exp2((near_peak - peak) * RATE)
        c = jnp.exp2((far_peak - peak) * RATE)
        share = 1.0 / (near_total * a + far_total * c)
        acc[h] = acc[h] * (a * share)
        far_stat[h] = jnp.broadcast_to(c * share, (TOK, HEAD_DIM))
        return carry

    lax.fori_loop(0, HEADS, factors, 0)

    def o_copy(h):
        cols = pl.ds(pl.multiple_of(h * HEAD_DIM, HEAD_DIM), HEAD_DIM)
        return pltpu.make_async_copy(o_heads.at[h], o.at[:, cols], os.at[h])

    def far_values(h, carry):
        for b in range(BLOCKS):
            rows = slice(b * BLOCK, (b + 1) * BLOCK)
            vals = jnp.concatenate(
                [far_v[jnp.maximum(lists[b * NFAR + n], 0), h] for n in SLOTS], axis=0)
            far_out = jnp.dot(weight[h, b], vals, preferred_element_type=jnp.float32)
            o_heads[h, rows] = (acc[h, rows] + far_out * far_stat[h, rows]).astype(jnp.bfloat16)
        o_copy(h).start()
        return carry

    arrived(0)
    lax.fori_loop(0, HEADS, far_values, 0)

    for t in range(2):
        for s in range(SIDE):
            @pl.when(jnp.logical_and(z - s >= 0, z < SIDE - 1))
            def _():
                z_copy(t, z - s, s, True).wait_send()

            @pl.when(jnp.logical_and(z + s < SIDE, z > 0))
            def _():
                z_copy(t, z + s, s, False).wait_send()

        for way in (0, 1):
            @pl.when(over[way])
            def _():
                near_copy(t, way).wait_send()

            @pl.when(jnp.logical_and(over[way], z != goal[way]))
            def _():
                last_copy(t, way).wait_send()
    for st in order:
        sent(*st, 0).wait()
        sent(*st, 1).wait()
    for h in range(HEADS):
        o_copy(h).wait()


def spread(query, key, value, q_gain, k_gain, far_pick, lists):
    vmem = pl.BlockSpec(memory_space=pltpu.VMEM)
    hbm = pl.BlockSpec(memory_space=pl.ANY)
    smem = pl.BlockSpec(memory_space=pltpu.SMEM)
    dma = pltpu.SemaphoreType.DMA
    bf, f32 = jnp.bfloat16, jnp.float32
    heads = (HEADS, TOK, HEAD_DIM)
    far = (FRAMES, HEADS, BLOCK, HEAD_DIM)
    return pl.pallas_call(
        spread_kernel,
        out_shape=jax.ShapeDtypeStruct((TOK, WIDTH), bf),
        in_specs=[hbm] * 3 + [vmem] * 2 + [smem] * 2,
        out_specs=hbm,
        scratch_shapes=[
            pltpu.VMEM((TOK, WIDTH), bf),
            pltpu.VMEM((TOK, WIDTH), bf),
            pltpu.VMEM(heads, bf),
            pltpu.VMEM(heads, f32),
            pltpu.VMEM(heads, f32),
            pltpu.VMEM((2, SIDE) + heads, bf),
            pltpu.VMEM((SIDE, 2, PEERS, HEADS, BLOCK, HEAD_DIM), bf),
            pltpu.VMEM((2, SIDE, HEADS, BLOCK, HEAD_DIM), bf),
            pltpu.VMEM((2, 2, HEADS, 2 * BLOCK, HEAD_DIM), bf),
            pltpu.VMEM((2,) + heads, bf),
            pltpu.VMEM((8, TOK), f32),
            pltpu.VMEM((GROUPS, 8, TOK), f32),
            pltpu.VMEM(far, bf),
            pltpu.VMEM(far, bf),
            pltpu.VMEM((HEADS, BLOCKS, BLOCK, FARK), bf),
            pltpu.VMEM(heads, f32),
            pltpu.VMEM(heads, bf),
            dma((2 + HEADS,)),
            dma((2, SIDE, 2)), dma((SIDE, 2)),
            dma((SIDE, 2, 2)), dma((SIDE, 2)),
            dma((2, 2)), dma((2, 2)), dma((2, 2)), dma((2,)),
            dma((GROUPS,)), dma((GROUPS,)),
            dma((SIDE, 2)), dma((HEADS,)),
        ],
        compiler_params=pltpu.CompilerParams(
            collective_id=0, has_side_effects=True, vmem_limit_bytes=60 << 20),
    )(query, key, value, q_gain, k_gain, far_pick, lists)


def local(query, key, value, q_gain, k_gain, far_frames, far_pick):
    frame = lax.axis_index("tm")
    mine = lax.dynamic_slice_in_dim(far_frames, frame * BLOCKS, BLOCKS, 0)
    return spread(query, key, value, q_gain, k_gain, far_pick, mine.reshape(-1))


def solution(mesh):
    placed = (P("tm", "head"), P("tm", "head"), P("tm", "head"), P("head"), P("head"), P(), P())
    return jax.shard_map(
        local, mesh=mesh, in_specs=placed, out_specs=P("tm", "head"), check_vma=False
    )
```

```python
import functools

import jax
import jax.numpy as jnp
from jax import lax
from jax.experimental import pallas as pl
from jax.experimental.pallas import tpu as pltpu
from jax.sharding import PartitionSpec as P

HEAD_DIM = 128
BLOCK = 64
NFAR = 12
SIDE = 4
HEADS = 5
BLOCKS = 8
FRAMES = 64
GROUPS = 8
TOK = BLOCK * BLOCKS
WIDTH = HEADS * HEAD_DIM
FULL = WIDTH * GROUPS
SLOTS = (0, 1, 2, 3, 4, 6, 7, 8, 9, 10)
FARK = len(SLOTS) * BLOCK
NEARK = 3 * TOK
epsilon = 1e-06
masked = -1e30
MESH = pl.DeviceIdType.MESH
PLANE = (
    (2, 2), (2, 1), (1, 2), (2, 3), (3, 2), (1, 1), (3, 3), (1, 3),
    (3, 1), (2, 0), (0, 2), (1, 0), (0, 1), (3, 0), (0, 3),
)
PEERS = len(PLANE)
ROWS = 256
RATE = HEAD_DIM ** (-0.5) * 1.4426950408889634
DIMS = (((1,), (1,)), ((), ()))


def spread_kernel(
    q, k, v, qg, kg, pick, lists, o,
    q_in, k_in, qn, acc, stat, zbuf, out, own, stage, nbuf, sums, parts, far_va, far_vb, far_k, weight, far_stat, o_heads,
    ins, zs, zr, fs, fr, ns, yr, cs, nr, hs, hr, ls, os,
):
    parts_of = (pl.ds(0, 3), pl.ds(3, HEADS - 3))
    frame = lax.axis_index("tm")
    group = lax.axis_index("head")
    col, z = frame // SIDE, frame % SIDE
    x, y = col // SIDE, col % SIDE

    def tm(dev):
        return {"tm": dev}

    def plane_peer(d):
        return (((x + d[0]) % SIDE) * SIDE + (y + d[1]) % SIDE) * SIDE + z

    def cut(h):
        return slice(h * HEAD_DIM, (h + 1) * HEAD_DIM)

    has_next, has_prev = col < 15, col > 0
    from_prev = jnp.logical_and(z == 0, has_prev)
    from_next = jnp.logical_and(z == SIDE - 1, has_next)

    loads = [pltpu.make_async_copy(q, q_in, ins.at[0]), pltpu.make_async_copy(k, k_in, ins.at[1])]
    loads += [pltpu.make_async_copy(v.at[:, cut(h)], zbuf.at[0, z, h], ins.at[2 + h]) for h in range(HEADS)]
    for c in loads:
        c.start()

    barrier = pltpu.get_barrier_semaphore()

    def greet(dev):
        pl.semaphore_signal(barrier, inc=1, device_id=dev, device_id_type=MESH)

    for d in PLANE:
        greet(tm(plane_peer(d)))
    for j in range(1, GROUPS):
        greet({"head": (group + j) % GROUPS})

    for j in range(1, SIDE):
        greet(tm(col * SIDE + (z + j) % SIDE))

    loads[0].wait()
    loads[1].wait()
    lane = lax.broadcasted_iota(jnp.int32, (TOK, HEAD_DIM), 1)
    q_part = jnp.sum(jnp.square(q_in[...].astype(jnp.float32)), axis=1, keepdims=True)
    k_part = jnp.sum(jnp.square(k_in[...].astype(jnp.float32)), axis=1, keepdims=True)
    both = jnp.where(lane == 0, q_part, jnp.where(lane == 1, k_part, 0.0))
    sums[...] = jnp.transpose(both)[:8]

    for c in loads[2:]:
        c.wait()
    pl.semaphore_wait(barrier, PEERS + GROUPS - 1 + SIDE - 1)

    sum_copies = []
    for j in range(1, GROUPS):
        c = pltpu.make_async_remote_copy(
            sums, parts.at[j], hs.at[j], hr.at[j],
            device_id={"head": (group + j) % GROUPS}, device_id_type=MESH)
        c.start()
        sum_copies.append(c)

    def z_copy(t, j, hop, right, h=None):
        dev = frame + 1 if right else frame - 1
        part = zbuf.at[t, j] if h is None else zbuf.at[t, j, h]
        return pltpu.make_async_remote_copy(
            part, part, zs.at[int(right), hop, t], zr.at[j, t],
            device_id=tm(dev), device_id_type=MESH)

    quarter = pl.ds(2 * BLOCK * z, 2 * BLOCK)
    over = (has_prev, has_next)
    goal = (0, SIDE - 1)

    def near_copy(t, up, h=None):
        heads = slice(None) if h is None else h
        return pltpu.make_async_remote_copy(
            zbuf.at[t, SIDE - 1 if up else 0, heads, quarter], stage.at[1 - up, t, heads],
            ns.at[up, t], yr.at[1 - up, t],
            device_id=tm(frame + SIDE if up else frame - SIDE), device_id_type=MESH)

    def cross(t, late):
        for h in range(HEADS):
            for up in (1, 0):
                outer = z == (0 if up else SIDE - 1)

                @pl.when(jnp.logical_and(over[up], outer if late else jnp.logical_not(outer)))
                def _():
                    near_copy(t, up, h).start()

    def last_copy(t, way):
        return pltpu.make_async_remote_copy(
            stage.at[way, t], nbuf.at[t, :, quarter], cs.at[way, t], nr.at[t],
            device_id=tm(col * SIDE + goal[way]), device_id_type=MESH)

    def deliver(t):
        for way in (0, 1):
            @pl.when(over[way])
            def _():
                pltpu.make_async_copy(stage.at[way, t], stage.at[way, t], yr.at[way, t]).wait()

                @pl.when(z != goal[way])
                def _():
                    last_copy(t, way).start()

                @pl.when(z == goal[way])
                def _():
                    pltpu.make_async_copy(stage.at[way, t], nbuf.at[t, :, quarter], nr.at[t]).start()

    def step_frame(s):
        if s == 0:
            return z
        if s == SIDE - 1:
            return jnp.where(z < 2, SIDE - 1, 0)
        table = {1: (1, 0, 3, 2), 2: (2, 2, 1, 1)}[s]
        r = jnp.int32(table[0])
        for i in range(1, SIDE):
            r = jnp.where(z == i, table[i], r)
        return r

    def landing(t, part, g):
        return (far_va, far_vb)[part].at[g] if t == 0 else far_k.at[g, parts_of[part]]

    def far_copy(s, t, i, j, part):
        return pltpu.make_async_remote_copy(
            out.at[s, t, i, parts_of[part]], landing(t, part, col * SIDE + j),
            fs.at[s, t, part], fr.at[s, t, part],
            device_id=tm(plane_peer(PLANE[i])), device_id_type=MESH)

    def own_copy(s, t, part, j, g):
        return pltpu.make_async_copy(own.at[t, j, parts_of[part]], landing(t, part, g), ls.at[s, t, part])

    def sent(s, t, part):
        held = out.at[s, t, :, parts_of[part]]
        return pltpu.make_async_copy(held, held, fs.at[s, t, part])

    def arrive(s, t):
        @pl.when(z - s >= 0)
        def _():
            z_copy(t, z - s, s, True).wait_recv()

        @pl.when(z + s < SIDE)
        def _():
            z_copy(t, z + s, s, False).wait_recv()

    def column(s, t, h):
        @pl.when(jnp.logical_and(z - s >= 0, z < SIDE - 1))
        def _():
            z_copy(t, z - s, s, True, h).start()

        @pl.when(jnp.logical_and(z + s < SIDE, z > 0))
        def _():
            z_copy(t, z + s, s, False, h).start()

    def choose(s, t):
        j = step_frame(s)
        g = col * SIDE + j
        picks = [pick[plane_peer(d), g] for d in PLANE] + [pick[frame, g]]

        def one_head(h, carry):
            blocks = [zbuf[t, j, h, b * BLOCK:(b + 1) * BLOCK] for b in range(BLOCKS)]
            for i, p in enumerate(picks):
                level = blocks
                for bit in range(3):
                    odd = ((p // (1 << bit)) % 2) == 1
                    level = [jnp.where(odd, level[2 * m + 1], level[2 * m]) for m in range(len(level) // 2)]
                if i < PEERS:
                    out[s, t, i, h] = level[0]
                else:
                    own[t, j, h] = level[0]
            return carry

        lax.fori_loop(0, HEADS, one_head, 0)
        for part in (0, 1):
            own_copy(s, t, part, j, g).start()

    def post(s, t, part, beside=None):
        j = step_frame(s)
        for i in range(PEERS):
            far_copy(s, t, i, j, part).start()
            if beside is not None and i % 3 == 0:
                column(*beside, i // 3)

    for h in range(HEADS):
        column(0, 0, h)
    choose(0, 0)
    post(0, 0, 0)
    post(0, 0, 1)
    for c in sum_copies:
        c.wait()
    total = sums[...]
    for j in range(1, GROUPS):
        total = total + parts[j]
    total = jnp.concatenate([total, jnp.zeros((HEAD_DIM - 8, TOK), jnp.float32)], axis=0)
    scale = lax.rsqrt(jnp.transpose(total) / FULL + epsilon)
    q_scale, k_scale = scale[:, 0:1], scale[:, 1:2]
    for h in range(HEADS):
        k_norm = k_in[:, cut(h)].astype(jnp.float32) * k_scale * kg[cut(h)].reshape(1, HEAD_DIM)
        zbuf[1, z, h] = k_norm.astype(jnp.bfloat16)
    for h in range(HEADS):
        column(0, 1, h)
    for h in range(HEADS):
        qn[h] = (q_in[:, cut(h)].astype(jnp.float32) * q_scale * qg[cut(h)].reshape(1, HEAD_DIM)).astype(jnp.bfloat16)
    def near_rows(t, h):
        return jnp.concatenate(
            [zbuf[t, jnp.maximum(z - 1, 0), h], zbuf[t, z, h], zbuf[t, jnp.minimum(z + 1, SIDE - 1), h]], axis=0)

    place = lax.broadcasted_iota(jnp.int32, (1, NEARK), 1) // TOK
    near_ok = jnp.logical_and(
        jnp.logical_or(place > 0, z > 0), jnp.logical_or(place < 2, z < SIDE - 1))
    half_lane = lax.broadcasted_iota(jnp.int32, (ROWS, HEAD_DIM), 1) < BLOCK

    def near_tile(n, carry):
        h, i = n // (TOK // ROWS), n % (TOK // ROWS)
        rows = pl.ds(i * ROWS, ROWS)
        score = lax.dot_general(qn[h, rows], near_rows(1, h), DIMS, preferred_element_type=jnp.float32)
        score = jnp.where(near_ok, score, masked)
        peak = score.max(-1, keepdims=True)
        prob = jnp.exp2((score - peak) * RATE)
        total = prob.sum(-1, keepdims=True)
        acc[h, rows] = jnp.dot(
            prob.astype(jnp.bfloat16), near_rows(0, h), preferred_element_type=jnp.float32)
        stat[h, rows] = jnp.where(half_lane, peak, total)
        return carry

    order = [(0, 0), (0, 1), (1, 0), (1, 1), (2, 1), (2, 0), (3, 1), (3, 0)]
    for r in range(1, len(order)):
        s, t = order[r]
        beside = order[r + 1] if r + 1 < len(order) else None
        moves = beside is not None and beside[0] < SIDE - 1
        early = beside != (2, 1)
        choose(s, t)
        if beside is not None and early:
            arrive(*beside)
        post(s, t, 0, beside if moves and early else None)
        if beside is not None and not early:
            arrive(*beside)
        if r == 4:
            cross(1, False)
            cross(0, False)
        if r == 5:
            cross(1, True)
        if r == 6:
            cross(0, True)
        if r == 7:
            deliver(1)
        post(s, t, 1, beside if moves and not early else None)
        if r == 7:
            lax.fori_loop(0, HEADS * (TOK // ROWS), near_tile, 0)
    deliver(0)

    def arrived(t, part):
        for s in range(SIDE):
            own_copy(s, t, part, 0, 0).wait()
            held = out.at[s, t, :, parts_of[part]]
            pltpu.make_async_copy(held, held, fr.at[s, t, part]).wait()

    slot = lax.broadcasted_iota(jnp.int32, (1, FARK), 1) // BLOCK

    def far_scores(h, carry):
        scores = []
        for b in range(BLOCKS):
            sources = [lists[b * NFAR + n] for n in SLOTS]
            bias = jnp.zeros((1, FARK), jnp.float32)
            for n, g in enumerate(sources):
                bias = jnp.where(slot == n, jnp.where(g >= 0, 0.0, masked), bias)
            keys = jnp.concatenate([far_k[jnp.maximum(g, 0), h] for g in sources], axis=0)
            scores.append(lax.dot_general(
                qn[h, b * BLOCK:(b + 1) * BLOCK], keys, DIMS, preferred_element_type=jnp.float32) + bias)
        for b in range(BLOCKS):
            peak = scores[b].max(-1, keepdims=True)
            prob = jnp.exp2((scores[b] - peak) * RATE)
            weight[h, b] = prob.astype(jnp.bfloat16)
            far_stat[h, b * BLOCK:(b + 1) * BLOCK] = jnp.where(
                half_lane[:BLOCK], peak, prob.sum(-1, keepdims=True))
        return carry

    def cross_tile(n, carry):
        h, i = n // (TOK // ROWS), n % (TOK // ROWS)
        rows = pl.ds(i * ROWS, ROWS)
        score = lax.dot_general(qn[h, rows], nbuf[1, h], DIMS, preferred_element_type=jnp.float32)
        old_peak, old_total = stat[h, rows][:, 0:1], stat[h, rows][:, BLOCK:BLOCK + 1]
        peak = jnp.maximum(old_peak, score.max(-1, keepdims=True))
        prob = jnp.exp2((score - peak) * RATE)
        shrink = jnp.exp2((old_peak - peak) * RATE)
        total = old_total * shrink + prob.sum(-1, keepdims=True)
        acc[h, rows] = acc[h, rows] * shrink + jnp.dot(
            prob.astype(jnp.bfloat16), nbuf[0, h], preferred_element_type=jnp.float32)
        stat[h, rows] = jnp.where(half_lane, peak, total)
        return carry

    @pl.when(jnp.logical_or(from_prev, from_next))
    def _():
        for t in range(2):
            pltpu.make_async_copy(nbuf.at[t], nbuf.at[t], nr.at[t]).wait()
        lax.fori_loop(0, HEADS * (TOK // ROWS), cross_tile, 0)

    arrived(1, 0)
    arrived(1, 1)
    lax.fori_loop(0, HEADS, far_scores, 0)

    def factors(h, carry):
        near_peak, near_total = stat[h][:, 0:1], stat[h][:, BLOCK:BLOCK + 1]
        far_peak, far_total = far_stat[h][:, 0:1], far_stat[h][:, BLOCK:BLOCK + 1]
        peak = jnp.maximum(near_peak, far_peak)
        a = jnp.exp2((near_peak - peak) * RATE)
        c = jnp.exp2((far_peak - peak) * RATE)
        share = 1.0 / (near_total * a + far_total * c)
        acc[h] = acc[h] * (a * share)
        far_stat[h] = jnp.broadcast_to(c * share, (TOK, HEAD_DIM))
        return carry

    lax.fori_loop(0, HEADS, factors, 0)

    def o_copy(h):
        cols = pl.ds(pl.multiple_of(h * HEAD_DIM, HEAD_DIM), HEAD_DIM)
        return pltpu.make_async_copy(o_heads.at[h], o.at[:, cols], os.at[h])

    def far_values(held, first, h, carry):
        for b in range(BLOCKS):
            rows = slice(b * BLOCK, (b + 1) * BLOCK)
            vals = jnp.concatenate(
                [held[jnp.maximum(lists[b * NFAR + n], 0), h - first] for n in SLOTS], axis=0)
            far_out = jnp.dot(weight[h, b], vals, preferred_element_type=jnp.float32)
            o_heads[h, rows] = (acc[h, rows] + far_out * far_stat[h, rows]).astype(jnp.bfloat16)
        o_copy(h).start()
        return carry

    arrived(0, 0)
    lax.fori_loop(0, 3, functools.partial(far_values, far_va, 0), 0)
    arrived(0, 1)
    lax.fori_loop(3, HEADS, functools.partial(far_values, far_vb, 3), 0)

    for t in range(2):
        for s in range(SIDE):
            @pl.when(jnp.logical_and(z - s >= 0, z < SIDE - 1))
            def _():
                z_copy(t, z - s, s, True).wait_send()

            @pl.when(jnp.logical_and(z + s < SIDE, z > 0))
            def _():
                z_copy(t, z + s, s, False).wait_send()

        for way in (0, 1):
            @pl.when(over[way])
            def _():
                near_copy(t, way).wait_send()

            @pl.when(jnp.logical_and(over[way], z != goal[way]))
            def _():
                last_copy(t, way).wait_send()
    for st in order:
        sent(*st, 0).wait()
        sent(*st, 1).wait()
    for h in range(HEADS):
        o_copy(h).wait()


def spread(query, key, value, q_gain, k_gain, far_pick, lists):
    vmem = pl.BlockSpec(memory_space=pltpu.VMEM)
    hbm = pl.BlockSpec(memory_space=pl.ANY)
    smem = pl.BlockSpec(memory_space=pltpu.SMEM)
    dma = pltpu.SemaphoreType.DMA
    bf, f32 = jnp.bfloat16, jnp.float32
    heads = (HEADS, TOK, HEAD_DIM)
    far = (FRAMES, HEADS, BLOCK, HEAD_DIM)
    return pl.pallas_call(
        spread_kernel,
        out_shape=jax.ShapeDtypeStruct((TOK, WIDTH), bf),
        in_specs=[hbm] * 3 + [vmem] * 2 + [smem] * 2,
        out_specs=hbm,
        scratch_shapes=[
            pltpu.VMEM((TOK, WIDTH), bf),
            pltpu.VMEM((TOK, WIDTH), bf),
            pltpu.VMEM(heads, bf),
            pltpu.VMEM(heads, f32),
            pltpu.VMEM(heads, f32),
            pltpu.VMEM((2, SIDE) + heads, bf),
            pltpu.VMEM((SIDE, 2, PEERS, HEADS, BLOCK, HEAD_DIM), bf),
            pltpu.VMEM((2, SIDE, HEADS, BLOCK, HEAD_DIM), bf),
            pltpu.VMEM((2, 2, HEADS, 2 * BLOCK, HEAD_DIM), bf),
            pltpu.VMEM((2,) + heads, bf),
            pltpu.VMEM((8, TOK), f32),
            pltpu.VMEM((GROUPS, 8, TOK), f32),
            pltpu.VMEM((FRAMES, 3, BLOCK, HEAD_DIM), bf),
            pltpu.VMEM((FRAMES, HEADS - 3, BLOCK, HEAD_DIM), bf),
            pltpu.VMEM(far, bf),
            pltpu.VMEM((HEADS, BLOCKS, BLOCK, FARK), bf),
            pltpu.VMEM(heads, f32),
            pltpu.VMEM(heads, bf),
            dma((2 + HEADS,)),
            dma((2, SIDE, 2)), dma((SIDE, 2)),
            dma((SIDE, 2, 2)), dma((SIDE, 2, 2)),
            dma((2, 2)), dma((2, 2)), dma((2, 2)), dma((2,)),
            dma((GROUPS,)), dma((GROUPS,)),
            dma((SIDE, 2, 2)), dma((HEADS,)),
        ],
        compiler_params=pltpu.CompilerParams(
            collective_id=0, has_side_effects=True, vmem_limit_bytes=60 << 20),
    )(query, key, value, q_gain, k_gain, far_pick, lists)


def local(query, key, value, q_gain, k_gain, far_frames, far_pick):
    frame = lax.axis_index("tm")
    mine = lax.dynamic_slice_in_dim(far_frames, frame * BLOCKS, BLOCKS, 0)
    return spread(query, key, value, q_gain, k_gain, far_pick, mine.reshape(-1))


def solution(mesh):
    placed = (P("tm", "head"), P("tm", "head"), P("tm", "head"), P("head"), P("head"), P(), P())
    return jax.shard_map(
        local, mesh=mesh, in_specs=placed, out_specs=P("tm", "head"), check_vma=False
    )
```
